128 devices in a mesh: section: 2 (over z_lo), dp: 16 (over y, x), ctx: 4 (over z_hi, core).
Axes of the slice: x: 4, y: 4, z: 4 (z_hi: 2, z_lo: 2; z = z_hi * 2 + z_lo), core: 2. Of those that a mesh axis runs over, the one named last changes fastest.
Arguments:
- ends_in: bfloat16 [2, 2, 16, 512, 896], P('section', None, 'dp', 'ctx'), may hold values from -6 to 6
- segment_ids: int32 [2, 16, 512], P(None, 'dp', 'ctx'), may hold values from 0 to 3, as said below
- norm_gains: bfloat16 [2, 2, 896], P('section', None, ('dp', 'ctx')), may hold values from 0.25 to 1.75
- qkv_weight: bfloat16 [2, 896, 1152], P('section', ('dp', 'ctx')), may hold values from -1.6035675 to 1.6035675
- qkv_bias: bfloat16 [2, 1152], P('section', ('dp', 'ctx')), may hold values from -3 to 3
- out_weight: bfloat16 [2, 896, 896], P('section', ('dp', 'ctx')), may hold values from -0.1875 to 0.1875
- in_weight: bfloat16 [2, 896, 9728], P('section', ('dp', 'ctx')), may hold values from -0.1875 to 0.1875
- down_weight: bfloat16 [2, 4864, 896], P('section', ('dp', 'ctx')), may hold values from -0.15625 to 0.15625
Outputs:
- ends_out: float32 [2, 2, 16, 512, 896], P('section', None, 'dp', 'ctx')
- grad_gains: float32 [2, 2, 896], P('section', None, ('dp', 'ctx'))
- grad_qkv_weight: float32 [2, 896, 1152], P('section', ('dp', 'ctx'))
- grad_qkv_bias: float32 [2, 1152], P('section', ('dp', 'ctx'))
- grad_out_weight: float32 [2, 896, 896], P('section', ('dp', 'ctx'))
- grad_in_weight: float32 [2, 896, 9728], P('section', ('dp', 'ctx'))
- grad_down_weight: float32 [2, 4864, 896], P('section', ('dp', 'ctx'))
The draws below stay inside these ranges and needn't reach their ends.
Inputs may be any that keep to these rules, and one draw needn't show every extreme that they name: `segment_ids`: in every pack the ids start at 0 and never fall along the positions. Among the 2 x 1 packs that share an index of dp, one holds a document that begins within the first 128 positions and ends within the last 128.
All inputs are finite; a program needn't handle non-finite values.
Results may differ from the reference program's by a relative error of at most 0.03.
Values may be sent and summed in bfloat16 or wider, within the bound.
A program may use at most 192 MiB of HBM per device.

```python
import math
import jax
import jax.numpy as jnp
from jax import lax

D = 896
HEADS = 14
KV_HEADS = 2
HEAD = 64
FF = 4864
LEN = 512
MB = 2
SEQ_DP = 1
QKV = 1152
SHARD_LEN = 128
SEQS = 16
N_SECTION = 2


def draw_segment_ids(key, part):
    key = jax.random.fold_in(key, 7)
    cut_key, first_key, last_key, choose_key = jax.random.split(key, 4)
    cut_points = jax.random.randint(cut_key, (MB, SEQS, 3), 1, LEN)
    first_cut = jax.random.randint(first_key, (MB, SEQS), 1, SHARD_LEN)
    last_cut = jax.random.randint(last_key, (MB, SEQS), LEN - SHARD_LEN + 1, LEN)
    blocks = SEQS // SEQ_DP
    chosen = jax.random.randint(choose_key, (blocks,), 0, MB * SEQ_DP)
    micro_index = jnp.arange(MB, dtype=jnp.int32)[:, None]
    seq_index = jnp.arange(SEQS, dtype=jnp.int32)[None, :]
    slot_index = micro_index * SEQ_DP + seq_index % SEQ_DP
    spanning = slot_index == chosen[seq_index // SEQ_DP]
    special = jnp.stack([first_cut, last_cut, last_cut], axis=-1)
    cut_points = jnp.where(spanning[..., None], special, cut_points)
    positions = jnp.arange(LEN, dtype=jnp.int32)
    above = (positions[None, None, :, None] >= cut_points[:, :, None, :]).astype(jnp.int32)
    return jnp.sum(above, axis=-1).astype(jnp.int32)


def draw_qkv_weight(key, part):
    key = jax.random.fold_in(key, 11)
    entries = jnp.clip(jax.random.normal(key, (2, D, QKV), jnp.float32), -6.0, 6.0)
    columns = jnp.arange(QKV, dtype=jnp.int32)
    factor = jnp.where(columns >= (HEADS + KV_HEADS) * HEAD, 8.0, 1.0).astype(jnp.float32)
    return (entries * factor[None, None, :] * D ** (-0.5)).astype(jnp.bfloat16)


def level_of(key, shape, cuts, least, largest):
    def one(dim, parts):
        draws = jax.random.uniform(jax.random.fold_in(jax.random.fold_in(key, 6), dim), (parts,), jnp.float32, least / len(cuts), largest / len(cuts))
        return jnp.repeat(jnp.exp(draws), shape[dim] // parts).reshape((-1,) + (1,) * (len(shape) - dim - 1))

    loudness = one(*cuts[0])
    for cut in cuts[1:]:
        loudness = loudness * one(*cut)
    return loudness


def normal_values(key, shape, deviation, limit, cuts=(), kind=jnp.bfloat16):
    drawn = jax.random.normal(key, shape, jnp.float32) * deviation
    if len(cuts) > 0:
        drawn = level_of(key, shape, cuts, -0.22, 0.18) * drawn
    return jnp.clip(drawn, min=-limit, max=limit).astype(kind)


def setup_inputs(seed: int = 0) -> dict:
    keys = jax.random.split(jax.random.key(seed), 9)
    return {
        "ends_in": normal_values(keys[0], (2, MB, SEQS, LEN, D), 1.0, 6.0, ((0, 2), (2, 16), (3, 4))),
        "segment_ids": draw_segment_ids(jax.random.fold_in(keys[8], 71), 0),
        "norm_gains": jnp.clip(1.0 + 0.15 * jax.random.normal(keys[2], (N_SECTION, 2, D), jnp.float32), 0.25, 1.75).astype(jnp.bfloat16),
        "qkv_weight": draw_qkv_weight(jax.random.fold_in(keys[8], 71), 0),
        "qkv_bias": normal_values(keys[4], (N_SECTION, QKV), 0.5, 3.0, ((0, 2), (1, 64))),
        "out_weight": normal_values(keys[5], (N_SECTION, D, D), D ** -0.5, 0.1875, ((0, 2), (1, 64))),
        "in_weight": normal_values(keys[6], (N_SECTION, D, 2 * FF), D ** -0.5, 0.1875, ((0, 2), (1, 64))),
        "down_weight": normal_values(keys[7], (N_SECTION, FF, D), (FF // 4) ** -0.5, 0.15625, ((0, 2), (1, 64))),
    }


@jax.custom_vjp
def low(v):
    return lax.optimization_barrier(v.astype(jnp.bfloat16)).astype(jnp.float32)

@jax.custom_vjp
def low_back(v):
    return v

def low_keep(v):
    return (low(v), None)

def low_pass(kept, grad):
    return (grad,)

def back_keep(v):
    return (v, None)

def back_low(kept, grad):
    return (low(grad),)
low.defvjp(low_keep, low_pass)
low_back.defvjp(back_keep, back_low)
highest = lax.Precision.HIGHEST
epsilon = 1e-06
rope_base = 1000000.0
masked_score = -1000000000.0

def rms_scale(residual, gain_row):
    return residual * lax.rsqrt(lax.optimization_barrier(jnp.mean(residual * residual, axis=-1, keepdims=True)) + epsilon) * gain_row

def rotate(tensor, rope_cos, rope_sin):
    half_dim = tensor.shape[-1] // 2
    turned = jnp.concatenate([-tensor[..., half_dim:], tensor[..., :half_dim]], axis=-1)
    return tensor * rope_cos + turned * rope_sin

def rope_tables(segments):
    indices = jnp.arange(LEN, dtype=jnp.int32)
    starts_here = jnp.concatenate([jnp.ones((segments.shape[0], 1), dtype=bool), segments[:, 1:] != segments[:, :-1]], axis=1)
    doc_start = lax.cummax(jnp.where(starts_here, indices[None, :], 0), axis=1)
    positions = (indices[None, :] - doc_start).astype(jnp.float32)
    frequency = rope_base ** (-jnp.arange(0, HEAD, 2, dtype=jnp.float32) / HEAD)
    angles = positions[..., None] * frequency
    rope_cos = jnp.concatenate([jnp.cos(angles), jnp.cos(angles)], axis=-1)[:, :, None, :]
    rope_sin = jnp.concatenate([jnp.sin(angles), jnp.sin(angles)], axis=-1)[:, :, None, :]
    return (rope_cos, rope_sin)

def layer_block(residual, segments, rope_cos, rope_sin, weights):
    gain_pair, w_qkv, b_qkv, w_out, w_in, w_down = weights
    pack_count = residual.shape[0]
    q_width = HEADS * HEAD
    kv_width = KV_HEADS * HEAD
    group_size = HEADS // KV_HEADS
    normed = low(rms_scale(residual, gain_pair[0]))
    linear = low_back(jnp.einsum('pld,de->ple', normed, w_qkv, precision=highest) + b_qkv)
    query_lin = linear[..., :q_width].reshape(pack_count, LEN, HEADS, HEAD)
    key_lin = linear[..., q_width:q_width + kv_width].reshape(pack_count, LEN, KV_HEADS, HEAD)
    value_lin = linear[..., q_width + kv_width:].reshape(pack_count, LEN, KV_HEADS, HEAD)
    queries = low(rotate(query_lin, rope_cos, rope_sin) * HEAD ** (-0.5))
    key_rows = low(rotate(key_lin, rope_cos, rope_sin))
    values = low(value_lin)
    queries = queries.reshape(pack_count, LEN, KV_HEADS, group_size, HEAD)
    scores = low_back(jnp.einsum('pqgja,pkga->pgjqk', queries, key_rows, precision=highest))
    indices = jnp.arange(LEN)
    allowed = (segments[:, :, None] == segments[:, None, :]) & (indices[None, :] <= indices[:, None])
    scores = jnp.where(allowed[:, None, None], scores, masked_score)
    attn_probs = low(jax.nn.softmax(scores, axis=-1))
    attended = jnp.einsum('pgjqk,pkga->pqgja', attn_probs, values, precision=highest)
    attended = low_back(low(attended.reshape(pack_count, LEN, q_width)))
    middle = residual + low_back(jnp.einsum('ple,ed->pld', attended, w_out, precision=highest))
    normed_mid = low(rms_scale(middle, gain_pair[1]))
    gate_up = low_back(jnp.einsum('pld,df->plf', normed_mid, w_in, precision=highest))
    hidden = low(jax.nn.silu(gate_up[..., :FF]) * gate_up[..., FF:])
    return middle + low_back(jnp.einsum('plf,fd->pld', hidden, w_down, precision=highest))

def apply_layer(residual, segments, rope_cos, rope_sin, weights):
    pack_count = residual.shape[0]
    per_block = math.gcd(pack_count, 8)

    def blocked(tensor):
        return tensor.reshape((pack_count // per_block, per_block) + tensor.shape[1:])

    def one_block(operands):
        return layer_block(operands[0], operands[1], operands[2], operands[3], weights)
    outcome = lax.map(jax.checkpoint(one_block), (blocked(residual), blocked(segments), blocked(rope_cos), blocked(rope_sin)))
    return outcome.reshape(residual.shape)

def reference(ends_in, segment_ids, norm_gains, qkv_weight, qkv_bias, out_weight, in_weight, down_weight):
    pack_count = MB * SEQS
    segments = segment_ids.reshape(pack_count, LEN)
    rope_cos, rope_sin = rope_tables(segments)
    first_in = ends_in[0].astype(jnp.float32).reshape(pack_count, LEN, D)
    cotangent = ends_in[1].astype(jnp.float32).reshape(pack_count, LEN, D)
    params = (norm_gains.astype(jnp.float32), qkv_weight.astype(jnp.float32), qkv_bias.astype(jnp.float32), out_weight.astype(jnp.float32), in_weight.astype(jnp.float32), down_weight.astype(jnp.float32))

    def forward(residual, weights):
        for layer_idx in range(N_SECTION):
            if layer_idx > 0:
                residual = low_back(low(residual))
            residual = apply_layer(residual, segments, rope_cos, rope_sin, tuple((weight[layer_idx] for weight in weights)))
        return residual
    result, pullback = jax.vjp(forward, first_in, params)
    grad_first, grad_params = pullback(cotangent)
    ends_out = jnp.stack([grad_first, result]).reshape(2, MB, SEQS, LEN, D)
    grad_gains, grad_qkv_weight, grad_qkv_bias, grad_out_weight, grad_in_weight, grad_down_weight = grad_params
    return (ends_out, grad_gains, grad_qkv_weight, grad_qkv_bias, grad_out_weight, grad_in_weight, grad_down_weight)
```

```python
import jax
import jax.numpy as jnp
from jax import lax
from jax.experimental import pallas as pl
from jax.experimental.pallas import tpu as pltpu
from jax.sharding import PartitionSpec as P

MESH = pl.DeviceIdType.MESH
HEADS = 14
HEAD = 64
D = 896
DP = 1024
QKV = 1152
FF = 4864
FP = 5120
ROWS = 128
WIDE = 2 * FP + QKV + D
GATE = QKV + D
TILE = 512
EPS = 1e-06
BF = jnp.bfloat16
F32 = jnp.float32
ANY = pl.BlockSpec(memory_space=pl.ANY)
VM = pl.BlockSpec(memory_space=pltpu.VMEM)


def place():
    dp, ctx = lax.axis_index("dp"), lax.axis_index("ctx")
    core, zh = lax.rem(ctx, 2), ctx // 2
    y, x = dp // 4, lax.rem(dp, 4)
    one = core * y + (1 - core) * x
    two = core * x + (1 - core) * y
    return core, zh, one, two

def dp_at(core, one, two):
    return two * (4 - 3 * core) + one * (1 + 3 * core)

def ids(core, zh, one, two):
    return {"dp": dp_at(core, one, two), "ctx": 2 * zh + core}

def gather_kernel(wd, wn, gd, gn, send, recv, loc):
    core, zh, one, two = place()
    ring = lambda p: lax.rem(p + 8, 4)
    sib = {"dp": dp_at(core, one, two), "ctx": 2 * zh + 1 - core}
    zpart = ids(core, 1 - zh, one, two)
    barrier = pltpu.get_barrier_semaphore()
    for other in (sib, zpart, ids(core, zh, ring(one + 1), two), ids(core, zh, ring(one - 1), two),
                  ids(core, zh, one, ring(two + 1)), ids(core, zh, one, ring(two - 1))):
        pl.semaphore_signal(barrier, inc=1, device_id=other, device_id_type=MESH)
    pl.semaphore_wait(barrier, 6)
    hs = (zh, 1 - zh)
    started = []

    def shard(q1, q2, h):
        return 4 * dp_at(core, q1, q2) + 2 * h + core

    def copies(src, s, msg, dev):
        d0, n0 = src
        out = []
        for i, (a, g) in enumerate(((d0, gd), (n0, gn))):
            out.append(pltpu.make_async_remote_copy(src_ref=a, dst_ref=g.at[s], send_sem=send.at[2 * msg + i],
                       recv_sem=recv.at[2 * msg + i], device_id=dev, device_id_type=MESH))
        return out

    def go(src, s, msg, dev):
        for c in copies(src, s, msg, dev):
            c.start()
            started.append(c)

    def held(s):
        return gd.at[s], gn.at[s]

    def arrive(s, msg):
        for c in copies(held(s), s, msg, sib):
            c.wait_recv()

    A, B, D = 0, 1, 2
    m1 = lambda k, kind: 1 + 3 * k + kind
    m2 = lambda j, k, kind: 7 + (2 * j + k) * 3 + kind
    m3 = lambda j, k, t: 31 + (2 * j + k) * 4 + t

    own = shard(one, two, zh)
    lc = [pltpu.make_async_copy(wd, gd.at[own], loc.at[0]), pltpu.make_async_copy(wn, gn.at[own], loc.at[1])]
    for c in lc:
        c.start()

    dirs = [1 - 2 * h for h in hs]
    def pos(k, j, p):
        return ring(p + (0, -dirs[k], dirs[k], 2)[j])

    def spread(k, j, src):
        q1 = pos(k, j, one)
        s = shard(q1, two, hs[k])
        go(src, s, m2(j, k, A), ids(core, zh, one, ring(two + dirs[k])))
        go(src, s, m2(j, k, B), ids(core, zh, one, ring(two - dirs[k])))
        go(src, s, m3(j, k, 0), sib)

    def first(k, src):
        s = shard(one, two, hs[k])
        go(src, s, m1(k, A), ids(core, zh, ring(one + dirs[k]), two))
        go(src, s, m1(k, B), ids(core, zh, ring(one - dirs[k]), two))
        spread(k, 0, src)

    src = (wd, wn)
    go(src, own, 0, zpart)
    first(0, src)
    s = shard(one, two, hs[1])
    arrive(s, 0)
    first(1, held(s))
    for k in (0, 1):
        s = shard(pos(k, 1, one), two, hs[k])
        arrive(s, m1(k, A))
        go(held(s), s, m1(k, D), ids(core, zh, ring(one + dirs[k]), two))
        spread(k, 1, held(s))
        s = shard(pos(k, 2, one), two, hs[k])
        arrive(s, m1(k, B))
        spread(k, 2, held(s))
    for k in (0, 1):
        s = shard(pos(k, 3, one), two, hs[k])
        arrive(s, m1(k, D))
        spread(k, 3, held(s))
    for j in range(4):
        for k in (0, 1):
            q1 = pos(k, j, one)
            s = shard(q1, pos(k, 1, two), hs[k])
            arrive(s, m2(j, k, A))
            go(held(s), s, m2(j, k, D), ids(core, zh, one, ring(two + dirs[k])))
            go(held(s), s, m3(j, k, 1), sib)
            s = shard(q1, pos(k, 2, two), hs[k])
            arrive(s, m2(j, k, B))
            go(held(s), s, m3(j, k, 2), sib)
    for j in range(4):
        for k in (0, 1):
            s = shard(pos(k, j, one), pos(k, 3, two), hs[k])
            arrive(s, m2(j, k, D))
            go(held(s), s, m3(j, k, 3), sib)
    oc, o1, o2 = 1 - core, two, one
    for j in range(4):
        for k in (0, 1):
            for t in range(4):
                s = 4 * dp_at(oc, pos(k, j, o1), pos(k, t, o2)) + 2 * hs[k] + oc
                arrive(s, m3(j, k, t))
    for c in started:
        c.wait_send()
    for c in lc:
        c.wait()

def gather(wd, wn):
    return pl.pallas_call(
        gather_kernel,
        out_shape=(jax.ShapeDtypeStruct((64,) + wd.shape, wd.dtype), jax.ShapeDtypeStruct((64,) + wn.shape, wn.dtype)),
        in_specs=[pl.BlockSpec(memory_space=pl.ANY)] * 2,
        out_specs=(pl.BlockSpec(memory_space=pl.ANY),) * 2,
        scratch_shapes=[pltpu.SemaphoreType.DMA((126,)), pltpu.SemaphoreType.DMA((126,)), pltpu.SemaphoreType.DMA((2,))],
        compiler_params=pltpu.CompilerParams(collective_id=0, has_side_effects=True),
        name="gather",
    )(wd, wn)


def scatter_kernel(pd, pn, od, on, sd, sn, rd, rn, td, tn, fd, fn, send, recv, loc, oloc):
    core, zh, one, two = place()
    ring = lambda p: lax.rem(p + 8, 4)
    oc = 1 - core
    sib = {"dp": dp_at(core, one, two), "ctx": 2 * zh + oc}
    zpart = ids(core, 1 - zh, one, two)
    barrier = pltpu.get_barrier_semaphore()
    for other in (sib, zpart, ids(core, zh, ring(one + 1), two), ids(core, zh, ring(one - 1), two),
                  ids(core, zh, one, ring(two + 1)), ids(core, zh, one, ring(two - 1))):
        pl.semaphore_signal(barrier, inc=1, device_id=other, device_id_type=MESH)
    pl.semaphore_wait(barrier, 6)
    hs = (zh, 1 - zh)
    dirs = [1 - 2 * h for h in hs]
    started = []
    A, B, D = 0, 1, 2

    def copies(src, dst, msg, dev):
        return [pltpu.make_async_remote_copy(src_ref=a, dst_ref=g, send_sem=send.at[2 * msg + i],
                recv_sem=recv.at[2 * msg + i], device_id=dev, device_id_type=MESH)
                for i, (a, g) in enumerate(zip(src, dst))]

    def go(src, dst, msg, dev):
        for c in copies(src, dst, msg, dev):
            c.start()
            started.append(c)

    def arrive(dst, msg):
        for c in copies(dst, dst, msg, sib):
            c.wait_recv()

    def pos(k, j, p):
        return ring(p + (0, -dirs[k], dirs[k], 2)[j])

    def add(dst, src):
        def body(i, _):
            c = pl.ds(pl.multiple_of(i * 1024, 1024), 1024)
            dst[0][:, c] = dst[0][:, c] + src[0][:, c]
            return 0
        lax.fori_loop(0, 12, body, 0)
        dst[1][...] = dst[1][...] + src[1][...]

    order = [(j, k) for j in (3, 2, 1, 0) for k in (1, 0)]
    ts = (3, 2, 1, 0)
    sslot = lambda j, k, t: (2 * j + k) * 4 + t
    for j, k in order:
        for t in ts:
            s = 4 * dp_at(oc, pos(k, j, two), pos(k, t, one)) + 2 * hs[k] + oc
            n = sslot(j, k, t)
            go((pd.at[s], pn.at[s]), (sd.at[n], sn.at[n]), n, sib)
    m2 = lambda j, k, kind: 32 + (2 * j + k) * 3 + kind
    m1 = lambda k, kind: 56 + 3 * k + kind
    rslot = lambda m: (rd.at[m - 32], rn.at[m - 32])
    mz = 62

    flat = [(j, k, t) for j, k in order for t in ts]
    def fetch(n):
        j, k, t = flat[n]
        s = 4 * dp_at(core, pos(k, j, one), pos(k, t, two)) + 2 * hs[k] + core
        b = n % 4
        return [pltpu.make_async_copy(pd.at[s], td.at[b], loc.at[b, 0]), pltpu.make_async_copy(pn.at[s], tn.at[b], loc.at[b, 1])]
    for n in range(4):
        for c in fetch(n):
            c.start()

    def piece(n):
        j, k, t = flat[n]
        m = sslot(j, k, t)
        here = (sd.at[m], sn.at[m])
        for c in fetch(n):
            c.wait()
        arrive(here, m)
        add(here, (td.at[n % 4], tn.at[n % 4]))
        if n + 4 < len(flat):
            for c in fetch(n + 4):
                c.start()
        return here

    sums = {}
    def two_start(g):
        j, k = order[g]
        for i, t in enumerate(ts):
            here = piece(4 * g + i)
            sums[j, k, t] = here
            if t == 3:
                m = m2(j, k, D)
                go(here, rslot(m), m, ids(core, zh, one, ring(two - dirs[k])))
            if t == 2:
                m = m2(j, k, B)
                go(here, rslot(m), m, ids(core, zh, one, ring(two + dirs[k])))

    def two_mid(g):
        j, k = order[g]
        here = sums[j, k, 1]
        got = rslot(m2(j, k, D))
        arrive(got, m2(j, k, D))
        add(here, got)
        m = m2(j, k, A)
        go(here, rslot(m), m, ids(core, zh, one, ring(two - dirs[k])))

    def two_end(g):
        j, k = order[g]
        here = sums[j, k, 0]
        for kind in (B, A):
            got = rslot(m2(j, k, kind))
            arrive(got, m2(j, k, kind))
            add(here, got)
        if j == 3:
            m = m1(k, D)
            go(here, rslot(m), m, ids(core, zh, ring(one - dirs[k]), two))
        if j == 2:
            m = m1(k, B)
            go(here, rslot(m), m, ids(core, zh, ring(one + dirs[k]), two))
        if j == 1:
            got = rslot(m1(k, D))
            arrive(got, m1(k, D))
            add(here, got)
            m = m1(k, A)
            go(here, rslot(m), m, ids(core, zh, ring(one - dirs[k]), two))
        if j == 0:
            for kind in (B, A):
                got = rslot(m1(k, kind))
                arrive(got, m1(k, kind))
                add(here, got)
            if k == 1:
                go(here, rslot(mz), mz, zpart)
            else:
                got = rslot(mz)
                arrive(got, mz)
                def body(i, _):
                    c = pl.ds(pl.multiple_of(i * 1024, 1024), 1024)
                    fd[:, c] = here[0][:, c].astype(jnp.float32) + got[0][:, c].astype(jnp.float32)
                    return 0
                lax.fori_loop(0, 12, body, 0)
                fn[...] = here[1][...].astype(jnp.float32) + got[1][...].astype(jnp.float32)
                last = [pltpu.make_async_copy(fd, od, oloc.at[0]), pltpu.make_async_copy(fn, on, oloc.at[1])]
                for c in last:
                    c.start()
                for c in last:
                    c.wait()

    for step in range(len(order) + 2):
        if step < len(order):
            two_start(step)
        if 0 <= step - 1 < len(order):
            two_mid(step - 1)
        if 0 <= step - 2:
            two_end(step - 2)
    for c in started:
        c.wait_send()

def scatter(pd, pn):
    bf = jnp.bfloat16
    return pl.pallas_call(
        scatter_kernel,
        out_shape=(jax.ShapeDtypeStruct(pd.shape[1:], jnp.float32), jax.ShapeDtypeStruct(pn.shape[1:], jnp.float32)),
        in_specs=[pl.BlockSpec(memory_space=pl.ANY)] * 2,
        out_specs=(pl.BlockSpec(memory_space=pl.ANY),) * 2,
        scratch_shapes=[
            pltpu.VMEM((32, 16, 12288), bf), pltpu.VMEM((32, 80, 896), bf),
            pltpu.VMEM((31, 16, 12288), bf), pltpu.VMEM((31, 80, 896), bf),
            pltpu.VMEM((4, 16, 12288), bf), pltpu.VMEM((4, 80, 896), bf),
            pltpu.VMEM((16, 12288), jnp.float32), pltpu.VMEM((80, 896), jnp.float32),
            pltpu.SemaphoreType.DMA((126,)), pltpu.SemaphoreType.DMA((126,)), pltpu.SemaphoreType.DMA((4, 2)), pltpu.SemaphoreType.DMA((2,))],
        compiler_params=pltpu.CompilerParams(collective_id=1, has_side_effects=True, vmem_limit_bytes=50 * 2**20),
        name="scatter",
    )(pd, pn)


def nn(a, b):
    return jnp.dot(a, b, preferred_element_type=F32)


def nt(a, b):
    return lax.dot_general(a, b, (((1,), (1,)), ((), ())), preferred_element_type=F32)


def tn(a, b):
    return lax.dot_general(a, b, (((0,), (0,)), ((), ())), preferred_element_type=F32)


def unpad(v, spread):
    hi = v.astype(BF)
    lo = (v - hi.astype(F32)).astype(BF)
    return nt(hi, spread) + nt(lo, spread)


def rms(v):
    return lax.rsqrt(jnp.mean(v * v, axis=-1, keepdims=True) + EPS)


def rms_back(g_normed, v, gain):
    r = rms(v)
    n = v * r
    gg = g_normed * gain
    pulled = r * (gg - n * jnp.mean(gg * n, axis=-1, keepdims=True))
    return pulled, jnp.sum(g_normed * n, axis=0, keepdims=True)


def swap(u):
    width = u.shape[1]
    lane = lax.broadcasted_iota(jnp.int32, u.shape, 1)
    return jnp.where(lane % 64 < 32, pltpu.roll(u, width - 32, 1), pltpu.roll(u, 32, 1))


def wide(table, n):
    return jnp.concatenate([table] * n, axis=1)


def variants(kv):
    kv = kv.astype(F32)
    lo = lax.broadcasted_iota(jnp.int32, kv.shape, 1) < 64
    turned = pltpu.roll(kv, 64, 1)
    return [
        jnp.where(lo, kv, 0.0).astype(BF),
        jnp.where(lo, 0.0, turned).astype(BF),
        jnp.where(lo, turned, 0.0).astype(BF),
        jnp.where(lo, 0.0, kv).astype(BF),
    ]


GROUPS = ((0, 0, (0, 1, 2, 3)), (0, 1, (0, 1, 2)), (1, 0, (4, 5, 6)), (1, 1, (3, 4, 5, 6)))


def pairs(v, which):
    return jnp.concatenate([v[:, 128 * p : 128 * p + 128] for p in which], axis=0)


def allowed_mask(ids_own, ids_all, me):
    row = me * ROWS + lax.broadcasted_iota(jnp.int32, (ROWS, 4 * ROWS), 0)
    col = lax.broadcasted_iota(jnp.int32, (ROWS, 4 * ROWS), 1)
    return (ids_own == ids_all) & (col <= row)


def probs(q, k_var, mask, which):
    s = nt(pairs(q, which), k_var).reshape(len(which), ROWS, 4 * ROWS)
    s = jnp.where(mask[None], s, -1e9)
    e = jnp.exp(s - jnp.max(s, axis=-1, keepdims=True))
    p = e / jnp.sum(e, axis=-1, keepdims=True)
    return p.reshape(len(which) * ROWS, 4 * ROWS)


def greet(peers):
    barrier = pltpu.get_barrier_semaphore()
    for c in peers:
        pl.semaphore_signal(barrier, inc=1, device_id={"ctx": c}, device_id_type=MESH)
    pl.semaphore_wait(barrier, 3)


def attn_fwd_kernel(h, gain, bias, cos, sin, ids_own, ids_all, spread, gd, mid, a_out, q_out, kv_out, o_out,
                    wqkv, wout, kv, wsem, send, recv):
    me = lax.axis_index("ctx")
    peers = [lax.rem(me + d, 4) for d in (1, 2, 3)]
    loads = [pltpu.make_async_copy(gd.at[:, pl.ds(0, QKV)], wqkv, wsem.at[0]),
             pltpu.make_async_copy(gd.at[:, pl.ds(QKV, D)], wout, wsem.at[1])]
    for c in loads:
        c.start()
    greet(peers)
    x = h[...]
    a = (x * rms(x) * gain[...]).astype(BF)
    a = nn(a, spread[...]).astype(BF)
    a_out[...] = a
    loads[0].wait()
    lin = nn(a, wqkv[...]) + bias[...]
    qk = lin[:, :1024]
    qk = qk * wide(cos[...], 8) + swap(qk) * wide(sin[...], 8)
    q = (qk[:, :D] * HEAD**-0.5).astype(BF)
    q_out[...] = q
    kv[me] = jnp.concatenate([qk[:, D:], lin[:, 1024:]], axis=1).astype(BF)
    moves = [pltpu.make_async_remote_copy(src_ref=kv.at[me], dst_ref=kv.at[me], send_sem=send.at[d], recv_sem=recv.at[d],
                                          device_id={"ctx": c}, device_id_type=MESH) for d, c in enumerate(peers)]
    for m in moves:
        m.start()
    mask = allowed_mask(ids_own[...], ids_all[...], me)
    for m in moves:
        m.wait_recv()
    for m in moves:
        m.wait_send()
    full = kv[...].reshape(4 * ROWS, 256)
    kv_out[...] = full
    ks, vs = variants(full[:, :128]), variants(full[:, 128:])
    o = [jnp.zeros((ROWS, 128), F32)] * 7
    for g, par, which in GROUPS:
        p = probs(q, ks[2 * g + par], mask, which).astype(BF)
        part = nn(p, vs[2 * g + par])
        for i, w in enumerate(which):
            o[w] = o[w] + part[i * ROWS : (i + 1) * ROWS]
    o = nn(jnp.concatenate(o, axis=1).astype(BF), spread[...]).astype(BF)
    o_out[...] = o
    loads[1].wait()
    mid[...] = x + nn(o, wout[...])


def attn_fwd(h, gain, bias, cos, sin, ids_own, ids_all, spread, gd):
    sds = jax.ShapeDtypeStruct
    return pl.pallas_call(
        attn_fwd_kernel,
        out_shape=(sds((ROWS, D), F32), sds((ROWS, DP), BF), sds((ROWS, D), BF), sds((4 * ROWS, 256), BF), sds((ROWS, DP), BF)),
        in_specs=[VM] * 8 + [ANY],
        out_specs=(VM,) * 5,
        scratch_shapes=[pltpu.VMEM((DP, QKV), BF), pltpu.VMEM((DP, D), BF), pltpu.VMEM((4, ROWS, 256), BF),
                        pltpu.SemaphoreType.DMA((2,)), pltpu.SemaphoreType.DMA((3,)), pltpu.SemaphoreType.DMA((3,))],
        compiler_params=pltpu.CompilerParams(collective_id=2, has_side_effects=True, vmem_limit_bytes=48 * 2**20),
        name="attn_fwd",
    )(h, gain, bias, cos, sin, ids_own, ids_all, spread, gd)


def attn_bwd_kernel(gmid, h, q_ref, kv_ref, gain, cos, sin, ids_own, ids_all, spread, gd,
                    gh, gh_low, glin_out, gz_out, ggain, gbias, wqkv, wout, part, got, wsem, send, recv):
    me = lax.axis_index("ctx")
    peers = [lax.rem(me + d, 4) for d in (1, 2, 3)]
    loads = [pltpu.make_async_copy(gd.at[:, pl.ds(0, QKV)], wqkv, wsem.at[0]),
             pltpu.make_async_copy(gd.at[:, pl.ds(QKV, D)], wout, wsem.at[1])]
    for c in loads:
        c.start()
    greet(peers)
    gm = gmid[...]
    gz = gm.astype(BF)
    gz_out[...] = gz
    loads[1].wait()
    go = nt(nt(gz, wout[...]).astype(BF), spread[...]).astype(BF)
    q = q_ref[...]
    full = kv_ref[...]
    ks, vs = variants(full[:, :128]), variants(full[:, 128:])
    mask = allowed_mask(ids_own[...], ids_all[...], me)
    gq = [jnp.zeros((ROWS, 128), F32)] * 7
    gk, gv = [], []
    for g, par, which in GROUPS:
        p = probs(q, ks[2 * g + par], mask, which)
        go_here = pairs(go, which)
        gp = nt(go_here, vs[2 * g + par])
        gv.append(tn(p.astype(BF), go_here))
        gs = (p * (gp - jnp.sum(p * gp, axis=-1, keepdims=True))).astype(BF)
        gk.append(tn(gs, pairs(q, which)))
        back = nn(gs, ks[2 * g + par])
        for i, w in enumerate(which):
            gq[w] = gq[w] + back[i * ROWS : (i + 1) * ROWS]
    lo = lax.broadcasted_iota(jnp.int32, (4 * ROWS, 128), 1) < 64

    def merged(e0, o0, e1, o1):
        return jnp.where(lo, e0, o1) + pltpu.roll(jnp.where(lo, e1, o0), 64, 1)

    part[...] = jnp.concatenate([merged(*gk), merged(*gv)], axis=1).reshape(4, ROWS, 256)
    moves = [pltpu.make_async_remote_copy(src_ref=part.at[c], dst_ref=got.at[d], send_sem=send.at[d], recv_sem=recv.at[d],
                                          device_id={"ctx": c}, device_id_type=MESH) for d, c in enumerate(peers)]
    for m in moves:
        m.start()
    cs, sn = cos[...], sin[...]
    gq = jnp.concatenate(gq, axis=1) * HEAD**-0.5
    gq = gq * wide(cs, 7) + swap(gq * wide(sn, 7))
    for m in moves:
        m.wait_recv()
    for m in moves:
        m.wait_send()
    own = part[me] + got[0] + got[1] + got[2]
    gk = own[:, :128]
    gk = gk * cs + swap(gk * sn)
    glin = jnp.concatenate([gq, gk, own[:, 128:]], axis=1).astype(BF)
    glin_out[...] = glin
    gbias[...] = jnp.sum(glin.astype(F32), axis=0, keepdims=True)
    loads[0].wait()
    ga = unpad(nt(glin, wqkv[...]), spread[...])
    pulled, gg = rms_back(ga, h[...], gain[...])
    ggain[...] = gg
    gh[...] = gm + pulled
    gh_low[...] = (gm + pulled).astype(BF)


def attn_bwd(gmid, h, q, kv, gain, cos, sin, ids_own, ids_all, spread, gd):
    sds = jax.ShapeDtypeStruct
    return pl.pallas_call(
        attn_bwd_kernel,
        out_shape=(sds((ROWS, D), F32), sds((ROWS, D), BF), sds((ROWS, QKV), BF), sds((ROWS, D), BF), sds((1, D), F32), sds((1, QKV), F32)),
        in_specs=[VM] * 10 + [ANY],
        out_specs=(VM,) * 6,
        scratch_shapes=[pltpu.VMEM((DP, QKV), BF), pltpu.VMEM((DP, D), BF), pltpu.VMEM((4, ROWS, 256), F32), pltpu.VMEM((3, ROWS, 256), F32),
                        pltpu.SemaphoreType.DMA((2,)), pltpu.SemaphoreType.DMA((3,)), pltpu.SemaphoreType.DMA((3,))],
        compiler_params=pltpu.CompilerParams(collective_id=3, has_side_effects=True, vmem_limit_bytes=48 * 2**20),
        name="attn_bwd",
    )(gmid, h, q, kv, gain, cos, sin, ids_own, ids_all, spread, gd)


def ffn_fwd_kernel(mid, gain, spread, wg, wu, wd, y, y_low, b_out, gate, up, m_out, acc):
    i = pl.program_id(0)

    @pl.when(i == 0)
    def _():
        v = mid[...]
        b_out[...] = nn((v * rms(v) * gain[...]).astype(BF), spread[...]).astype(BF)
        acc[...] = v

    b = b_out[...]
    gt, u = nn(b, wg[...]), nn(b, wu[...])
    gate[...] = gt.astype(BF)
    up[...] = u.astype(BF)
    m = (gt * jax.nn.sigmoid(gt) * u).astype(BF)
    m_out[...] = m
    acc[...] += nn(m, wd[...])

    @pl.when(i == pl.num_programs(0) - 1)
    def _():
        y[...] = acc[...]
        y_low[...] = acc[...].astype(BF)


def whole(shape):
    return pl.BlockSpec(shape, lambda i: (0, 0))


def ffn_fwd(mid, gain, spread, gd, gn):
    sds = jax.ShapeDtypeStruct
    steps = FP // TILE
    first = GATE // TILE
    cols = pl.BlockSpec((ROWS, TILE), lambda i: (0, i))
    return pl.pallas_call(
        ffn_fwd_kernel,
        grid=(steps,),
        out_shape=(sds((ROWS, D), F32), sds((ROWS, D), BF), sds((ROWS, DP), BF), sds((ROWS, FP), BF), sds((ROWS, FP), BF), sds((ROWS, FP), BF)),
        in_specs=[whole((ROWS, D)), whole((1, D)), whole((D, DP)),
                  pl.BlockSpec((DP, TILE), lambda i: (0, first + i)),
                  pl.BlockSpec((DP, TILE), lambda i: (0, first + steps + i)),
                  pl.BlockSpec((TILE, D), lambda i: (i, 0))],
        out_specs=(whole((ROWS, D)), whole((ROWS, D)), whole((ROWS, DP)), cols, cols, cols),
        scratch_shapes=[pltpu.VMEM((ROWS, D), F32)],
        compiler_params=pltpu.CompilerParams(vmem_limit_bytes=48 * 2**20),
        name="ffn_fwd",
    )(mid, gain, spread, gd, gd, gn)


def ffn_bwd_kernel(gy, mid, gain, spread, gate, up, wg, wu, wd, gmid, ggain, ggate, gup, acc):
    i = pl.program_id(0)

    @pl.when(i == 0)
    def _():
        acc[...] = jnp.zeros_like(acc)

    gm = nt(gy[...], wd[...])
    gt, u = gate[...].astype(F32), up[...].astype(F32)
    sg = jax.nn.sigmoid(gt)
    ggt = (gm * u * sg * (1.0 + gt * (1.0 - sg))).astype(BF)
    gu = (gm * gt * sg).astype(BF)
    ggate[...] = ggt
    gup[...] = gu
    acc[...] += nt(ggt, wg[...]) + nt(gu, wu[...])

    @pl.when(i == pl.num_programs(0) - 1)
    def _():
        pulled, gg = rms_back(unpad(acc[...], spread[...]), mid[...], gain[...])
        gmid[...] = gy[...].astype(F32) + pulled
        ggain[...] = gg


def ffn_bwd(gy, mid, gain, spread, gate, up, gd, gn):
    sds = jax.ShapeDtypeStruct
    steps = FP // TILE
    first = GATE // TILE
    cols = pl.BlockSpec((ROWS, TILE), lambda i: (0, i))
    return pl.pallas_call(
        ffn_bwd_kernel,
        grid=(steps,),
        out_shape=(sds((ROWS, D), F32), sds((1, D), F32), sds((ROWS, FP), BF), sds((ROWS, FP), BF)),
        in_specs=[whole((ROWS, D)), whole((ROWS, D)), whole((1, D)), whole((D, DP)), cols, cols,
                  pl.BlockSpec((DP, TILE), lambda i: (0, first + i)),
                  pl.BlockSpec((DP, TILE), lambda i: (0, first + steps + i)),
                  pl.BlockSpec((TILE, D), lambda i: (i, 0))],
        out_specs=(whole((ROWS, D)), whole((1, D)), cols, cols),
        scratch_shapes=[pltpu.VMEM((ROWS, DP), F32)],
        compiler_params=pltpu.CompilerParams(vmem_limit_bytes=48 * 2**20),
        name="ffn_bwd",
    )(gy, mid, gain, spread, gate, up, gd, gd, gn)


def wgrad_kernel(a, o, b, r, out):
    i = pl.program_id(0)

    @pl.when(i < 2)
    def _():
        out[...] = tn(a[...], r[...]).astype(BF)

    @pl.when(i == 2)
    def _():
        out[:, :128] = tn(a[...], r[:, :128]).astype(BF)
        out[:, 128:] = tn(o[...], r[:, 128:]).astype(BF)

    @pl.when(i == 3)
    def _():
        out[...] = tn(o[...], r[...]).astype(BF)

    @pl.when(i > 3)
    def _():
        out[...] = tn(b[...], r[...]).astype(BF)


def wgrad(a, o, b, r):
    tok = a.shape[0]
    return pl.pallas_call(
        wgrad_kernel,
        grid=(WIDE // TILE,),
        out_shape=jax.ShapeDtypeStruct((DP, WIDE), BF),
        in_specs=[whole((tok, DP))] * 3 + [pl.BlockSpec((tok, TILE), lambda i: (0, i))],
        out_specs=pl.BlockSpec((DP, TILE), lambda i: (0, i)),
        compiler_params=pltpu.CompilerParams(vmem_limit_bytes=48 * 2**20),
        name="wgrad",
    )(a, o, b, r)


def wgrad_down_kernel(m, gy, out):
    out[...] = tn(m[...], gy[...]).astype(BF)


def wgrad_down(m, gy):
    tok = m.shape[0]
    return pl.pallas_call(
        wgrad_down_kernel,
        grid=(FP // TILE,),
        out_shape=jax.ShapeDtypeStruct((FP, D), BF),
        in_specs=[pl.BlockSpec((tok, TILE), lambda i: (0, i)), whole((tok, D))],
        out_specs=pl.BlockSpec((TILE, D), lambda i: (i, 0)),
        compiler_params=pltpu.CompilerParams(vmem_limit_bytes=48 * 2**20),
        name="wgrad_down",
    )(m, gy)


def per_device(ends_in, segment_ids, norm_gains, qkv_weight, qkv_bias, out_weight, in_weight, down_weight):
    section = lax.axis_index("section")
    me = lax.axis_index("ctx")
    lead = in_weight[0].reshape(14, 2, 64, 76)
    lead = jnp.pad(lead, ((0, 0), (0, 0), (0, 0), (0, 4))).reshape(14, 2 * FP)
    rows = jnp.concatenate([qkv_weight[0], out_weight[0], lead], axis=1)
    pad = lambda v, n: jnp.pad(v, (0, n - v.shape[0]))
    extra = jnp.concatenate([pad(norm_gains[0, 0], 128), pad(norm_gains[0, 1], 128), pad(qkv_bias[0], WIDE - 256)])
    wd = jnp.concatenate([rows, extra[None], jnp.zeros((1, WIDE), BF)], axis=0)
    wn = jnp.pad(down_weight[0], ((0, 4), (0, 0)))
    gd, gn = gather(wd, wn)
    gains = [gd[:, 14, 128 * i : 128 * i + 14].reshape(1, D).astype(F32) for i in (0, 1)]
    bias = gd[:, 14, 256:274].reshape(1, QKV).astype(F32)
    gd, gn = gd.reshape(DP, WIDE), gn.reshape(FP, D)
    src = jnp.arange(D)
    spread = ((src + 2 * (src // 14))[:, None] == jnp.arange(DP)[None, :]).astype(BF)

    ids = lax.all_gather(segment_ids[:, 0], "ctx", axis=1, tiled=True)
    at = jnp.arange(4 * ROWS, dtype=jnp.int32)
    own_at = me * ROWS + at[:ROWS]
    same = (segment_ids[:, 0, :, None] == ids[:, None, :]) & (at[None, None, :] <= own_at[None, :, None])
    pos = (jnp.sum(same.astype(jnp.int32), axis=2) - 1).astype(F32)
    freq = 1000000.0 ** (-jnp.arange(0, HEAD, 2, dtype=F32) / HEAD)
    angle = pos[..., None] * freq
    c, s = jnp.cos(angle), jnp.sin(angle)
    cos = jnp.concatenate([c, c, c, c], axis=-1)
    sin = jnp.concatenate([-s, s, -s, s], axis=-1)

    def slot(t):
        return jnp.clip(t - section, 0, 1)

    def of(v, i):
        return lax.dynamic_index_in_dim(v, i, 0, keepdims=False)

    def place_of(t):
        i = slot(t)
        return of(cos, i), of(sin, i), of(segment_ids[:, 0], i)[:, None], of(ids, i)[None]

    kept = []
    incoming = None
    for t in range(3):
        h = ends_in[0, min(t, 1), 0].astype(F32)
        if t:
            h = jnp.where(section == 0, h, incoming.astype(F32))
        tables = place_of(t)
        mid, a, q, kv, o = attn_fwd(h, gains[0], bias, *tables, spread, gd)
        y, y_low, b, gate, up, m = ffn_fwd(mid, gains[1], spread, gd, gn)
        if t < 2:
            incoming = lax.ppermute(y_low, "section", [(0, 1)])
        kept.append((h, mid, a, q, kv, o, y, b, gate, up, m, tables))
    back = [None] * 3
    for u in range(3):
        t = 2 - u
        h, mid, a, q, kv, o, y, b, gate, up, m, tables = kept[t]
        first = ends_in[0, max(1 - u, 0), 0]
        here = incoming if u else jnp.zeros_like(first)
        if u == 2:
            first = jnp.zeros_like(first)
        gy = jnp.where(section == 1, first, here)
        gmid, gg1, ggate, gup = ffn_bwd(gy, mid, gains[1], spread, gate, up, gd, gn)
        gh, gh_low, glin, gz, gg0, gb = attn_bwd(gmid, h, q, kv, gains[0], *tables, spread, gd)
        if u < 2:
            incoming = lax.ppermute(gh_low, "section", [(1, 0)])
        back[t] = (gh, gy, ggate, gup, glin, gz, gg0, gg1, gb)

    def both(f):
        return jnp.concatenate([f(1), jnp.where(section == 0, f(0), f(2))], axis=0)

    a, o, b, m = (both(lambda t, i=i: kept[t][i]) for i in (2, 5, 7, 10))
    r = both(lambda t: jnp.concatenate([back[t][4], back[t][5], back[t][2], back[t][3]], axis=1))
    gy = both(lambda t: back[t][1])
    pd = wgrad(a, o, b, r).reshape(64, 16, WIDE)
    pn = wgrad_down(m, gy).reshape(64, 80, D)
    gg0, gg1, gb = (back[0][i] + back[1][i] + back[2][i] for i in (6, 7, 8))
    cell = lambda v: jnp.pad(v.reshape(64, -1), ((0, 0), (0, 128 - v.shape[1] // 64)))
    small = jnp.pad(jnp.concatenate([cell(gg0), cell(gg1), cell(gb)], axis=1), ((0, 0), (0, D - 384)))
    pn = lax.dynamic_update_slice(pn, small.astype(BF)[:, None], (0, 76, 0))
    sd, sn = scatter(pd, pn)
    ends = jnp.stack([jnp.where(section == 0, back[i][0], kept[i + 1][6]) for i in (0, 1)])
    g_in = sd[:14, GATE:].reshape(14, 2, 64, 80)[..., :76].reshape(14, 2 * FF)
    return (
        ends[None, :, None],
        jnp.stack([sn[76, :14], sn[76, 128:142]])[None],
        sd[None, :14, :QKV],
        sn[None, 76, 256:274],
        sd[None, :14, QKV:GATE],
        g_in[None],
        sn[None, :76],
    )


def solution(mesh):
    both = ("dp", "ctx")
    ends = P("section", None, "dp", "ctx", None)
    weights = (P("section", None, both), P("section", both, None), P("section", both), P("section", both, None),
               P("section", both, None), P("section", both, None))
    return jax.shard_map(per_device, mesh=mesh, in_specs=(ends, P(None, "dp", "ctx")) + weights,
                         out_specs=(ends,) + weights, check_vma=False)
```

```python
import jax
import jax.numpy as jnp
from jax import lax
from jax.experimental import pallas as pl
from jax.experimental.pallas import tpu as pltpu
from jax.sharding import PartitionSpec as P

MESH = pl.DeviceIdType.MESH
HEADS = 14
HEAD = 64
D = 896
DP = 1024
QKV = 1152
FF = 4864
FP = 5120
PACKS = 2
ROWS = 128
TOK = PACKS * ROWS
WIDE = 2 * FP + QKV + D
GATE = QKV + D
TILE = 1024
EPS = 1e-06
BF = jnp.bfloat16
F32 = jnp.float32
ANY = pl.BlockSpec(memory_space=pl.ANY)
VM = pl.BlockSpec(memory_space=pltpu.VMEM)


def place():
    dp, ctx = lax.axis_index("dp"), lax.axis_index("ctx")
    core, zh = lax.rem(ctx, 2), ctx // 2
    y, x = dp // 4, lax.rem(dp, 4)
    one = core * y + (1 - core) * x
    two = core * x + (1 - core) * y
    return core, zh, one, two

def dp_at(core, one, two):
    return two * (4 - 3 * core) + one * (1 + 3 * core)

def ids(core, zh, one, two):
    return {"dp": dp_at(core, one, two), "ctx": 2 * zh + core}

def gather_kernel(wd, wn, gd, gn, send, recv, loc):
    core, zh, one, two = place()
    ring = lambda p: lax.rem(p + 8, 4)
    sib = {"dp": dp_at(core, one, two), "ctx": 2 * zh + 1 - core}
    zpart = ids(core, 1 - zh, one, two)
    barrier = pltpu.get_barrier_semaphore()
    for other in (sib, zpart, ids(core, zh, ring(one + 1), two), ids(core, zh, ring(one - 1), two),
                  ids(core, zh, one, ring(two + 1)), ids(core, zh, one, ring(two - 1))):
        pl.semaphore_signal(barrier, inc=1, device_id=other, device_id_type=MESH)
    pl.semaphore_wait(barrier, 6)
    hs = (zh, 1 - zh)
    started = []

    def shard(q1, q2, h):
        return 4 * dp_at(core, q1, q2) + 2 * h + core

    def copies(src, s, msg, dev):
        d0, n0 = src
        out = []
        for i, (a, g) in enumerate(((d0, gd), (n0, gn))):
            out.append(pltpu.make_async_remote_copy(src_ref=a, dst_ref=g.at[s], send_sem=send.at[2 * msg + i],
                       recv_sem=recv.at[2 * msg + i], device_id=dev, device_id_type=MESH))
        return out

    def go(src, s, msg, dev):
        for c in copies(src, s, msg, dev):
            c.start()
            started.append(c)

    def held(s):
        return gd.at[s], gn.at[s]

    def arrive(s, msg):
        for c in copies(held(s), s, msg, sib):
            c.wait_recv()

    A, B, D = 0, 1, 2
    m1 = lambda k, kind: 1 + 3 * k + kind
    m2 = lambda j, k, kind: 7 + (2 * j + k) * 3 + kind
    m3 = lambda j, k, t: 31 + (2 * j + k) * 4 + t

    own = shard(one, two, zh)
    lc = [pltpu.make_async_copy(wd, gd.at[own], loc.at[0]), pltpu.make_async_copy(wn, gn.at[own], loc.at[1])]
    for c in lc:
        c.start()

    dirs = [1 - 2 * h for h in hs]
    def pos(k, j, p):
        return ring(p + (0, -dirs[k], dirs[k], 2)[j])

    def spread(k, j, src):
        q1 = pos(k, j, one)
        s = shard(q1, two, hs[k])
        go(src, s, m2(j, k, A), ids(core, zh, one, ring(two + dirs[k])))
        go(src, s, m2(j, k, B), ids(core, zh, one, ring(two - dirs[k])))
        go(src, s, m3(j, k, 0), sib)

    def first(k, src):
        s = shard(one, two, hs[k])
        go(src, s, m1(k, A), ids(core, zh, ring(one + dirs[k]), two))
        go(src, s, m1(k, B), ids(core, zh, ring(one - dirs[k]), two))
        spread(k, 0, src)

    src = (wd, wn)
    go(src, own, 0, zpart)
    first(0, src)
    s = shard(one, two, hs[1])
    arrive(s, 0)
    first(1, held(s))
    for k in (0, 1):
        s = shard(pos(k, 1, one), two, hs[k])
        arrive(s, m1(k, A))
        go(held(s), s, m1(k, D), ids(core, zh, ring(one + dirs[k]), two))
        spread(k, 1, held(s))
        s = shard(pos(k, 2, one), two, hs[k])
        arrive(s, m1(k, B))
        spread(k, 2, held(s))
    for k in (0, 1):
        s = shard(pos(k, 3, one), two, hs[k])
        arrive(s, m1(k, D))
        spread(k, 3, held(s))
    for j in range(4):
        for k in (0, 1):
            q1 = pos(k, j, one)
            s = shard(q1, pos(k, 1, two), hs[k])
            arrive(s, m2(j, k, A))
            go(held(s), s, m2(j, k, D), ids(core, zh, one, ring(two + dirs[k])))
            go(held(s), s, m3(j, k, 1), sib)
            s = shard(q1, pos(k, 2, two), hs[k])
            arrive(s, m2(j, k, B))
            go(held(s), s, m3(j, k, 2), sib)
    for j in range(4):
        for k in (0, 1):
            s = shard(pos(k, j, one), pos(k, 3, two), hs[k])
            arrive(s, m2(j, k, D))
            go(held(s), s, m3(j, k, 3), sib)
    oc, o1, o2 = 1 - core, two, one
    for j in range(4):
        for k in (0, 1):
            for t in range(4):
                s = 4 * dp_at(oc, pos(k, j, o1), pos(k, t, o2)) + 2 * hs[k] + oc
                arrive(s, m3(j, k, t))
    for c in started:
        c.wait_send()
    for c in lc:
        c.wait()

def gather(wd, wn):
    return pl.pallas_call(
        gather_kernel,
        out_shape=(jax.ShapeDtypeStruct((64,) + wd.shape, wd.dtype), jax.ShapeDtypeStruct((64,) + wn.shape, wn.dtype)),
        in_specs=[pl.BlockSpec(memory_space=pl.ANY)] * 2,
        out_specs=(pl.BlockSpec(memory_space=pl.ANY),) * 2,
        scratch_shapes=[pltpu.SemaphoreType.DMA((126,)), pltpu.SemaphoreType.DMA((126,)), pltpu.SemaphoreType.DMA((2,))],
        compiler_params=pltpu.CompilerParams(collective_id=0, has_side_effects=True),
        name="gather",
    )(wd, wn)


def nn(a, b):
    return jnp.dot(a, b, preferred_element_type=F32)


def nt(a, b):
    return lax.dot_general(a, b, (((1,), (1,)), ((), ())), preferred_element_type=F32)


def tn(a, b):
    return lax.dot_general(a, b, (((0,), (0,)), ((), ())), preferred_element_type=F32)


def unpad(v, spread):
    hi = v.astype(BF)
    lo = (v - hi.astype(F32)).astype(BF)
    return nt(hi, spread) + nt(lo, spread)


def rms(v):
    return lax.rsqrt(jnp.mean(v * v, axis=-1, keepdims=True) + EPS)


def rms_back(g_normed, v, gain):
    r = rms(v)
    n = v * r
    gg = g_normed * gain
    pulled = r * (gg - n * jnp.mean(gg * n, axis=-1, keepdims=True))
    return pulled, jnp.sum(g_normed * n, axis=0, keepdims=True)


def swap(u):
    width = u.shape[1]
    lane = lax.broadcasted_iota(jnp.int32, u.shape, 1)
    return jnp.where(lane % 64 < 32, pltpu.roll(u, width - 32, 1), pltpu.roll(u, 32, 1))


def wide(table, n):
    return jnp.concatenate([table] * n, axis=1)


def variants(kv):
    kv = kv.astype(F32)
    lo = lax.broadcasted_iota(jnp.int32, kv.shape, 1) < 64
    turned = pltpu.roll(kv, 64, 1)
    return [
        jnp.where(lo, kv, 0.0).astype(BF),
        jnp.where(lo, 0.0, turned).astype(BF),
        jnp.where(lo, turned, 0.0).astype(BF),
        jnp.where(lo, 0.0, kv).astype(BF),
    ]


GROUPS = ((0, 0, (0, 1, 2, 3)), (0, 1, (0, 1, 2)), (1, 0, (4, 5, 6)), (1, 1, (3, 4, 5, 6)))


def pairs(v, which):
    return jnp.concatenate([v[:, 128 * p : 128 * p + 128] for p in which], axis=0)


def allowed_mask(ids_own, ids_all, me):
    row = me * ROWS + lax.broadcasted_iota(jnp.int32, (ROWS, 4 * ROWS), 0)
    col = lax.broadcasted_iota(jnp.int32, (ROWS, 4 * ROWS), 1)
    return (ids_own == ids_all) & (col <= row)


def probs(q, k_var, mask, which):
    s = nt(pairs(q, which), k_var).reshape(len(which), ROWS, 4 * ROWS)
    s = jnp.where(mask[None], s, -1e9)
    e = jnp.exp(s - jnp.max(s, axis=-1, keepdims=True))
    p = e / jnp.sum(e, axis=-1, keepdims=True)
    return p.reshape(len(which) * ROWS, 4 * ROWS)


def greet(peers):
    barrier = pltpu.get_barrier_semaphore()
    for c in peers:
        pl.semaphore_signal(barrier, inc=1, device_id={"ctx": c}, device_id_type=MESH)
    pl.semaphore_wait(barrier, 3)


def attn_fwd_kernel(h, gain, bias, cos, sin, ids_own, ids_all, spread, gd, mid, a_out, q_out, kv_out, o_out,
                    wqkv, wout, kv, wsem, send, recv):
    me = lax.axis_index("ctx")
    peers = [lax.rem(me + d, 4) for d in (1, 2, 3)]
    loads = [pltpu.make_async_copy(gd.at[:, pl.ds(0, QKV)], wqkv, wsem.at[0]),
             pltpu.make_async_copy(gd.at[:, pl.ds(QKV, D)], wout, wsem.at[1])]
    for c in loads:
        c.start()
    greet(peers)
    x = h[...]
    a = (x * rms(x) * gain[...]).astype(BF)
    a = nn(a, spread[...]).astype(BF)
    a_out[...] = a
    loads[0].wait()
    lin = nn(a, wqkv[...]) + bias[...]
    qk = lin[:, :1024]
    qk = qk * wide(cos[...], 8) + swap(qk) * wide(sin[...], 8)
    q = (qk[:, :D] * HEAD**-0.5).astype(BF)
    q_out[...] = q
    kv[me] = jnp.concatenate([qk[:, D:], lin[:, 1024:]], axis=1).astype(BF)
    moves = [pltpu.make_async_remote_copy(src_ref=kv.at[me], dst_ref=kv.at[me], send_sem=send.at[d], recv_sem=recv.at[d],
                                          device_id={"ctx": c}, device_id_type=MESH) for d, c in enumerate(peers)]
    for m in moves:
        m.start()
    for m in moves:
        m.wait_recv()
    for m in moves:
        m.wait_send()
    rows = []
    for pack in range(PACKS):
        here = slice(pack * ROWS, (pack + 1) * ROWS)
        mask = allowed_mask(ids_own[here, :], ids_all[pack : pack + 1, :], me)
        full = kv[:, here, :].reshape(4 * ROWS, 256)
        kv_out[pack] = full
        ks, vs = variants(full[:, :128]), variants(full[:, 128:])
        o = [jnp.zeros((ROWS, 128), F32)] * 7
        for g, par, which in GROUPS:
            p = probs(q[here], ks[2 * g + par], mask, which).astype(BF)
            part = nn(p, vs[2 * g + par])
            for i, w in enumerate(which):
                o[w] = o[w] + part[i * ROWS : (i + 1) * ROWS]
        rows.append(jnp.concatenate(o, axis=1).astype(BF))
    o = nn(jnp.concatenate(rows, axis=0), spread[...]).astype(BF)
    o_out[...] = o
    loads[1].wait()
    mid[...] = x + nn(o, wout[...])


def attn_fwd(h, gain, bias, cos, sin, ids_own, ids_all, spread, gd):
    sds = jax.ShapeDtypeStruct
    return pl.pallas_call(
        attn_fwd_kernel,
        out_shape=(sds((TOK, D), F32), sds((TOK, DP), BF), sds((TOK, D), BF), sds((PACKS, 4 * ROWS, 256), BF), sds((TOK, DP), BF)),
        in_specs=[VM] * 8 + [ANY],
        out_specs=(VM,) * 5,
        scratch_shapes=[pltpu.VMEM((DP, QKV), BF), pltpu.VMEM((DP, D), BF), pltpu.VMEM((4, TOK, 256), BF),
                        pltpu.SemaphoreType.DMA((2,)), pltpu.SemaphoreType.DMA((3,)), pltpu.SemaphoreType.DMA((3,))],
        compiler_params=pltpu.CompilerParams(collective_id=2, has_side_effects=True, vmem_limit_bytes=48 * 2**20),
        name="attn_fwd",
    )(h, gain, bias, cos, sin, ids_own, ids_all, spread, gd)


def attn_back(gmid, q_ref, kv_ref, cos, sin, ids_own, ids_all, spread, wout, part, got, send, recv, me, peers, load):
    gz = gmid[...].astype(BF)
    load.wait()
    go = nt(nt(gz, wout[...]).astype(BF), spread[...]).astype(BF)
    yield gz
    q = q_ref[...]
    lo = lax.broadcasted_iota(jnp.int32, (4 * ROWS, 128), 1) < 64

    def merged(e0, o0, e1, o1):
        return jnp.where(lo, e0, o1) + pltpu.roll(jnp.where(lo, e1, o0), 64, 1)

    rows = []
    for pack in range(PACKS):
        here = slice(pack * ROWS, (pack + 1) * ROWS)
        full = kv_ref[pack]
        ks, vs = variants(full[:, :128]), variants(full[:, 128:])
        mask = allowed_mask(ids_own[here, :], ids_all[pack : pack + 1, :], me)
        gq = [jnp.zeros((ROWS, 128), F32)] * 7
        gk, gv = [], []
        for n, (g, par, which) in enumerate(GROUPS):
            p = probs(q[here], ks[2 * g + par], mask, which)
            go_here = pairs(go[here], which)
            gp = nt(go_here, vs[2 * g + par])
            gv.append(tn(p.astype(BF), go_here))
            gs = (p * (gp - jnp.sum(p * gp, axis=-1, keepdims=True))).astype(BF)
            gk.append(tn(gs, pairs(q[here], which)))
            back = nn(gs, ks[2 * g + par])
            for i, w in enumerate(which):
                gq[w] = gq[w] + back[i * ROWS : (i + 1) * ROWS]
            if n == 3:
                part[:, here, :] = jnp.concatenate([merged(*gk), merged(*gv)], axis=1).reshape(4, ROWS, 256)
                rows.append(jnp.concatenate(gq, axis=1))
                if pack == PACKS - 1:
                    moves = [pltpu.make_async_remote_copy(src_ref=part.at[c], dst_ref=got.at[d], send_sem=send.at[d], recv_sem=recv.at[d],
                                                          device_id={"ctx": c}, device_id_type=MESH) for d, c in enumerate(peers)]
                    for m in moves:
                        m.start()
            yield None
    cs, sn = cos[...], sin[...]
    gq = jnp.concatenate(rows, axis=0) * HEAD**-0.5
    gq = gq * wide(cs, 7) + swap(gq * wide(sn, 7))
    for m in moves:
        m.wait_recv()
    for m in moves:
        m.wait_send()
    own = part[me] + got[0] + got[1] + got[2]
    gk = own[:, :128]
    gk = gk * cs + swap(gk * sn)
    yield jnp.concatenate([gq, gk, own[:, 128:]], axis=1).astype(BF)


def attn_bwd_kernel(gmid, h, q_ref, kv_ref, gain, cos, sin, ids_own, ids_all, spread, gd,
                    gh_low, glin_out, gz_out, ggain, gbias, wqkv, wout, part, got, wsem, send, recv):
    me = lax.axis_index("ctx")
    peers = [lax.rem(me + d, 4) for d in (1, 2, 3)]
    loads = [pltpu.make_async_copy(gd.at[:, pl.ds(0, QKV)], wqkv, wsem.at[0]),
             pltpu.make_async_copy(gd.at[:, pl.ds(QKV, D)], wout, wsem.at[1])]
    for c in loads:
        c.start()
    greet(peers)
    found = list(attn_back(gmid, q_ref, kv_ref, cos, sin, ids_own, ids_all, spread, wout, part, got, send, recv, me, peers, loads[1]))
    gz_out[...] = found[0]
    glin = found[-1]
    glin_out[...] = glin
    gbias[...] = jnp.sum(glin.astype(F32), axis=0, keepdims=True)
    loads[0].wait()
    ga = unpad(nt(glin, wqkv[...]), spread[...])
    pulled, gg = rms_back(ga, h[...], gain[...])
    ggain[...] = gg
    gh_low[...] = (gmid[...] + pulled).astype(BF)


def attn_bwd(gmid, h, q, kv, gain, cos, sin, ids_own, ids_all, spread, gd):
    sds = jax.ShapeDtypeStruct
    return pl.pallas_call(
        attn_bwd_kernel,
        out_shape=(sds((TOK, D), BF), sds((TOK, QKV), BF), sds((TOK, D), BF), sds((1, D), F32), sds((1, QKV), F32)),
        in_specs=[VM] * 10 + [ANY],
        out_specs=(VM,) * 5,
        scratch_shapes=[pltpu.VMEM((DP, QKV), BF), pltpu.VMEM((DP, D), BF), pltpu.VMEM((4, TOK, 256), F32), pltpu.VMEM((3, TOK, 256), F32),
                        pltpu.SemaphoreType.DMA((2,)), pltpu.SemaphoreType.DMA((3,)), pltpu.SemaphoreType.DMA((3,))],
        compiler_params=pltpu.CompilerParams(collective_id=3, has_side_effects=True, vmem_limit_bytes=48 * 2**20),
        name="attn_bwd",
    )(gmid, h, q, kv, gain, cos, sin, ids_own, ids_all, spread, gd)


def ffn_fwd_kernel(mid, gain, spread, wg, wu, wd, y, y_low, b_out, gate, up, m_out, acc):
    i = pl.program_id(0)

    @pl.when(i == 0)
    def _():
        v = mid[...]
        b_out[...] = nn((v * rms(v) * gain[...]).astype(BF), spread[...]).astype(BF)
        acc[...] = v

    b = b_out[...]
    gt, u = nn(b, wg[...]), nn(b, wu[...])
    gate[...] = gt.astype(BF)
    up[...] = u.astype(BF)
    m = (gt * jax.nn.sigmoid(gt) * u).astype(BF)
    m_out[...] = m
    acc[...] += nn(m, wd[...])

    @pl.when(i == pl.num_programs(0) - 1)
    def _():
        y[...] = acc[...]
        y_low[...] = acc[...].astype(BF)


def whole(shape):
    return pl.BlockSpec(shape, lambda i: (0, 0))


def ffn_fwd(mid, gain, spread, gd, gn):
    sds = jax.ShapeDtypeStruct
    steps = FP // TILE
    first = GATE // TILE
    cols = pl.BlockSpec((TOK, TILE), lambda i: (0, i))
    return pl.pallas_call(
        ffn_fwd_kernel,
        grid=(steps,),
        out_shape=(sds((TOK, D), F32), sds((TOK, D), BF), sds((TOK, DP), BF), sds((TOK, FP), BF), sds((TOK, FP), BF), sds((TOK, FP), BF)),
        in_specs=[whole((TOK, D)), whole((1, D)), whole((D, DP)),
                  pl.BlockSpec((DP, TILE), lambda i: (0, first + i)),
                  pl.BlockSpec((DP, TILE), lambda i: (0, first + steps + i)),
                  pl.BlockSpec((TILE, D), lambda i: (i, 0))],
        out_specs=(whole((TOK, D)), whole((TOK, D)), whole((TOK, DP)), cols, cols, cols),
        scratch_shapes=[pltpu.VMEM((TOK, D), F32)],
        compiler_params=pltpu.CompilerParams(vmem_limit_bytes=48 * 2**20),
        name="ffn_fwd",
    )(mid, gain, spread, gd, gd, gn)


def ffn_bwd_kernel(gy, mid, gain, spread, gate, up, wg, wu, wd, gmid, ggain, ggate, gup, acc):
    i = pl.program_id(0)

    @pl.when(i == 0)
    def _():
        acc[...] = jnp.zeros_like(acc)

    gm = nt(gy[...], wd[...])
    gt, u = gate[...].astype(F32), up[...].astype(F32)
    sg = jax.nn.sigmoid(gt)
    ggt = (gm * u * sg * (1.0 + gt * (1.0 - sg))).astype(BF)
    gu = (gm * gt * sg).astype(BF)
    ggate[...] = ggt
    gup[...] = gu
    acc[...] += nt(ggt, wg[...]) + nt(gu, wu[...])

    @pl.when(i == pl.num_programs(0) - 1)
    def _():
        pulled, gg = rms_back(unpad(acc[...], spread[...]), mid[...], gain[...])
        gmid[...] = gy[...].astype(F32) + pulled
        ggain[...] = gg


def ffn_bwd(gy, mid, gain, spread, gate, up, gd, gn):
    sds = jax.ShapeDtypeStruct
    steps = FP // TILE
    first = GATE // TILE
    cols = pl.BlockSpec((TOK, TILE), lambda i: (0, i))
    return pl.pallas_call(
        ffn_bwd_kernel,
        grid=(steps,),
        out_shape=(sds((TOK, D), F32), sds((1, D), F32), sds((TOK, FP), BF), sds((TOK, FP), BF)),
        in_specs=[whole((TOK, D)), whole((TOK, D)), whole((1, D)), whole((D, DP)), cols, cols,
                  pl.BlockSpec((DP, TILE), lambda i: (0, first + i)),
                  pl.BlockSpec((DP, TILE), lambda i: (0, first + steps + i)),
                  pl.BlockSpec((TILE, D), lambda i: (i, 0))],
        out_specs=(whole((TOK, D)), whole((1, D)), cols, cols),
        scratch_shapes=[pltpu.VMEM((TOK, DP), F32)],
        compiler_params=pltpu.CompilerParams(vmem_limit_bytes=48 * 2**20),
        name="ffn_bwd",
    )(gy, mid, gain, spread, gate, up, gd, gd, gn)


KINDS = 63
HELD = 16


class Reduction:
    def __init__(self, where, own, other, work, staged, rings, send, recv, fetched, chunks):
        self.core, self.zh, self.one, self.two = where
        self.own, self.other, self.work, self.staged, self.rings = own, other, work, staged, rings
        self.send, self.recv, self.fetched, self.chunks = send, recv, fetched, chunks
        self.hs = (self.zh, 1 - self.zh)
        self.dirs = [1 - 2 * h for h in self.hs]
        self.sib = {"dp": dp_at(self.core, self.one, self.two), "ctx": 2 * self.zh + 1 - self.core}
        self.zpart = ids(self.core, 1 - self.zh, self.one, self.two)
        self.order = [(j, k) for j in (3, 2, 1, 0) for k in (1, 0)]
        self.kinds = (3, 2, 1, 0)
        self.flat = [(j, k, t) for j, k in self.order for t in self.kinds]
        self.slots = work[0].shape[0]
        self.started, self.busy, self.sums = [], {}, {}

    def pos(self, k, j, p):
        return lax.rem(p + (0, -self.dirs[k], self.dirs[k], 2)[j] + 8, 4)

    def to_one(self, k, sign):
        return ids(self.core, self.zh, lax.rem(self.one + sign * self.dirs[k] + 8, 4), self.two)

    def to_two(self, k, sign):
        return ids(self.core, self.zh, self.one, lax.rem(self.two + sign * self.dirs[k] + 8, 4))

    def copies(self, src, dst, msg, dev):
        n = len(self.rings)
        return [pltpu.make_async_remote_copy(src_ref=a, dst_ref=g, send_sem=self.send.at[n * msg + i],
                recv_sem=self.recv.at[n * msg + i], device_id=dev, device_id_type=MESH)
                for i, (a, g) in enumerate(zip(src, dst))]

    def go(self, src, dst, msg, dev, n=None):
        made = self.copies(src, dst, msg, dev)
        for c in made:
            c.start()
        if n is None:
            self.started += made
        else:
            self.busy[n] = made

    def arrive(self, dst, msg):
        for c in self.copies(dst, dst, msg, self.sib):
            c.wait_recv()

    def add(self, dst, src):
        for d, s, step in zip(dst, src, self.chunks):
            if step is None:
                d[...] = d[...] + s[...]
                continue
            def body(i, _, d=d, s=s, step=step):
                c = pl.ds(pl.multiple_of(i * step, step), step)
                d[:, c] = d[:, c] + s[:, c]
                return 0
            lax.fori_loop(0, d.shape[1] // step, body, 0)

    def at(self, bufs, i):
        return [b.at[i] for b in bufs]

    def sslot(self, j, k, t):
        return (2 * j + k) * 4 + t

    def m2(self, j, k, kind):
        return 32 + (2 * j + k) * 3 + kind

    def m1(self, k, kind):
        return 56 + 3 * k + kind

    def ring(self, m):
        return self.at(self.rings, m - 32)

    def give(self):
        oc = 1 - self.core
        for j, k, t in self.flat:
            s = 4 * dp_at(oc, self.pos(k, j, self.two), self.pos(k, t, self.one)) + 2 * self.hs[k] + oc
            n = self.sslot(j, k, t)
            self.go(self.own(s), self.at(self.other, n), n, self.sib)

    def fetch(self, n):
        j, k, t = self.flat[n]
        s = 4 * dp_at(self.core, self.pos(k, j, self.one), self.pos(k, t, self.two)) + 2 * self.hs[k] + self.core
        got = self.at(self.other, self.sslot(j, k, t))
        b = n % 2
        out = []
        for i in range(len(self.rings)):
            out.append(pltpu.make_async_copy(self.own(s)[i], self.work[i].at[n % self.slots], self.fetched.at[b, 2 * i]))
            out.append(pltpu.make_async_copy(got[i], self.staged[i].at[b], self.fetched.at[b, 2 * i + 1]))
        return out

    def begin(self, n):
        for c in self.busy.pop(n - self.slots, ()):
            c.wait_send()
        self.arrive(self.at(self.other, self.sslot(*self.flat[n])), self.sslot(*self.flat[n]))
        for c in self.fetch(n):
            c.start()

    def piece(self, n):
        if n == 0:
            self.begin(0)
        if n + 1 < 32:
            self.begin(n + 1)
        for c in self.fetch(n):
            c.wait()
        here = self.at(self.work, n % self.slots)
        self.add(here, self.at(self.staged, n % 2))
        self.sums[self.flat[n]] = (here, n)
        return here

    def two_start(self, g):
        j, k = self.order[g]
        for i, t in enumerate(self.kinds):
            n = 4 * g + i
            here = self.piece(n)
            if t == 3:
                self.go(here, self.ring(self.m2(j, k, 2)), self.m2(j, k, 2), self.to_two(k, -1), n)
            if t == 2:
                self.go(here, self.ring(self.m2(j, k, 1)), self.m2(j, k, 1), self.to_two(k, 1), n)

    def two_mid(self, g):
        j, k = self.order[g]
        here, n = self.sums[j, k, 1]
        got = self.ring(self.m2(j, k, 2))
        self.arrive(got, self.m2(j, k, 2))
        self.add(here, got)
        self.go(here, self.ring(self.m2(j, k, 0)), self.m2(j, k, 0), self.to_two(k, -1), n)

    def two_end(self, g):
        j, k = self.order[g]
        here, n = self.sums[j, k, 0]
        for kind in (1, 0):
            got = self.ring(self.m2(j, k, kind))
            self.arrive(got, self.m2(j, k, kind))
            self.add(here, got)
        if j == 3:
            self.go(here, self.ring(self.m1(k, 2)), self.m1(k, 2), self.to_one(k, -1), n)
        if j == 2:
            self.go(here, self.ring(self.m1(k, 1)), self.m1(k, 1), self.to_one(k, 1), n)
        if j == 1:
            got = self.ring(self.m1(k, 2))
            self.arrive(got, self.m1(k, 2))
            self.add(here, got)
            self.go(here, self.ring(self.m1(k, 0)), self.m1(k, 0), self.to_one(k, -1), n)
        if j == 0:
            for kind in (1, 0):
                got = self.ring(self.m1(k, kind))
                self.arrive(got, self.m1(k, kind))
                self.add(here, got)
            if k == 1:
                self.go(here, self.ring(62), 62, self.zpart, n)
            else:
                got = self.ring(62)
                self.arrive(got, 62)
                self.result = (here, got)

    def step(self, i):
        if i < 8:
            self.two_start(i)
        if 0 <= i - 1 < 8:
            self.two_mid(i - 1)
        if 0 <= i - 2 < 8:
            self.two_end(i - 2)

    def finish(self):
        for c in self.started:
            c.wait_send()
        for made in self.busy.values():
            for c in made:
                c.wait_send()


WT = 512


def last_kernel(*refs):
    attn_in, ops, rest = refs[:11], refs[11:27], refs[27:]
    glin1, gz1, gg0_in, gg1_in, gb_in = ops[:5]
    a2, o2 = ops[5:7], ops[7:9]
    b2, m2, gate2, up2, gy2 = refs[20:22], refs[22:24], refs[24:26], refs[26:28], refs[28:30]
    (gh, g_qkv, g_out, g_in, g_down, g_rows, pd, pn, pa, hd, hn, ha) = refs[30:42]
    (wqkv, wout, part, got, wsem, asend, arecv, work_d, work_n, st_d, st_n, ring_d, ring_n, work_a, st_a, ring_a,
     lhs, rhs, vm, vgy, stage, stage_n, left, right, fsend, frecv, ffet, csend, crecv, cfet, psem, ssem, isem) = refs[42:]
    section, me = lax.axis_index("section"), lax.axis_index("ctx")
    where = core, zh, one, two = place()
    turn = lambda p: lax.rem(p + 8, 4)
    sib = {"dp": dp_at(core, one, two), "ctx": 2 * zh + 1 - core}
    zpart = ids(core, 1 - zh, one, two)
    diagonal = ids(1 - core, 1 - zh, two, one)
    barrier = pltpu.get_barrier_semaphore()
    for other in (sib, zpart, diagonal, ids(core, zh, turn(one + 1), two), ids(core, zh, turn(one - 1), two),
                  ids(core, zh, one, turn(two + 1)), ids(core, zh, one, turn(two - 1))):
        pl.semaphore_signal(barrier, inc=1, device_id=other, device_id_type=MESH)

    def mine(pairs_):
        for t in (0, 1):
            @pl.when(section == t)
            def _(t=t):
                for i, (src, dst, sem) in enumerate(pairs_):
                    pltpu.make_async_copy(src[t], dst, sem).start()

    def mine_wait(pairs_):
        for t in (0, 1):
            @pl.when(section == t)
            def _(t=t):
                for i, (src, dst, sem) in enumerate(pairs_):
                    pltpu.make_async_copy(src[t], dst, sem).wait()

    first = [(b2, lhs, psem.at[0]), (gate2, rhs.at[:, pl.ds(0, FP)], psem.at[1]), (up2, rhs.at[:, pl.ds(FP, FP)], psem.at[2])]
    second = [(m2, vm, psem.at[3]), (gy2, vgy, psem.at[4]), (a2, left.at[0], psem.at[5]), (o2, left.at[1], psem.at[6])]
    mine(first)
    mine(second)
    gmid, h, q_ref, kv_ref, gain, cos, sin, ids_own, ids_all, spread, gd = attn_in
    loads = [pltpu.make_async_copy(gd.at[:, pl.ds(0, QKV)], wqkv, wsem.at[0]),
             pltpu.make_async_copy(gd.at[:, pl.ds(QKV, D)], wout, wsem.at[1])]
    for c in loads:
        c.start()
    mine_wait(first)
    lt = lhs[...].T

    def write(i, b):
        at = i * WT if isinstance(i, int) else pl.multiple_of(i * WT, WT)
        return pltpu.make_async_copy(stage.at[b], pd.at[:, pl.ds(at, WT)], ssem.at[b])

    def tile(i, b):
        at = i * WT if isinstance(i, int) else pl.multiple_of(i * WT, WT)
        stage[b] = nn(lt, rhs[:, pl.ds(at, WT)]).astype(BF)
        write(i, b).start()

    steps = 2 * FP // WT
    for b in (0, 1):
        tile(b, b)

    def tiles(p, _):
        for b in (0, 1):
            write(2 * p + b - 2, b).wait()
            tile(2 * p + b, b)
        return 0
    lax.fori_loop(1, steps // 2, tiles, 0)
    mine_wait(second)

    def write_n(i, b):
        at = i * 640 if isinstance(i, int) else pl.multiple_of(i * 640, 640)
        return pltpu.make_async_copy(stage_n.at[b], pn.at[pl.ds(at, 640)], ssem.at[2 + b])

    def down(i, b):
        at = i * 640 if isinstance(i, int) else pl.multiple_of(i * 640, 640)
        stage_n[b] = tn(vm[:, pl.ds(at, 640)], vgy[...]).astype(BF)
        write_n(i, b).start()

    for b in (0, 1):
        down(b, b)

    def downs(p, _):
        for b in (0, 1):
            write_n(2 * p + b - 2, b).wait()
            down(2 * p + b, b)
        return 0
    lax.fori_loop(1, FP // 1280, downs, 0)
    for b in (0, 1):
        write(steps - 2 + b, b).wait()
        write_n(FP // 640 - 2 + b, b).wait()
    pl.semaphore_wait(barrier, 7)

    def own_f(s):
        return pd.at[pl.ds(pl.multiple_of(16 * s, 16), 16)], pn.at[pl.ds(pl.multiple_of(80 * s, 16), 80)]

    def own_a(s):
        return (pa.at[pl.ds(pl.multiple_of(16 * s, 16), 16)],)

    ffn = Reduction(where, own_f, (hd, hn), (work_d, work_n), (st_d, st_n), (ring_d, ring_n), fsend, frecv, ffet, (1024, None))
    att = Reduction(where, own_a, (ha,), (work_a,), (st_a,), (ring_a,), csend, crecv, cfet, (None,))
    ffn.give()

    peers = [lax.rem(me + d, 4) for d in (1, 2, 3)]
    body = attn_back(gmid, q_ref, kv_ref, cos, sin, ids_own, ids_all, spread, wout, part, got, asend, arecv, me, peers, loads[1])
    gz = next(body)

    def run(n):
        for _ in range(n):
            next(body)

    ffn.step(0)
    run(2)
    ffn.step(1)
    run(3)
    ffn.step(2)
    run(3)
    ffn.step(3)
    glin = next(body)
    loads[0].wait()
    ga = unpad(nt(glin, wqkv[...]), spread[...])
    pulled, gg0 = rms_back(ga, h[...], gain[...])
    gh[...] = gmid[...] + pulled
    gb = jnp.sum(glin.astype(F32), axis=0, keepdims=True) + gb_in[...]
    gg0 = gg0 + gg0_in[...]
    right[:, :QKV] = glin + glin1[...]
    right[:, QKV:] = gz + gz1[...]
    line = lax.broadcasted_iota(jnp.int32, (64, 16, 1), 1)
    mixed = tn(left[0], right[:, :QKV]).reshape(64, 16, QKV)
    stage_a = [mixed + jnp.where(line == 14, gb[None], 0.0)]
    mixed = tn(left[1], right[:, QKV:]).reshape(64, 16, D)
    stage_a.append(mixed + jnp.where(line == 14, gg0[None], 0.0) + jnp.where(line == 15, gg1_in[...][None], 0.0))
    whole_a = jnp.concatenate([v.reshape(DP, -1) for v in stage_a], axis=1).astype(BF)
    for i in range(4):
        stage[i % 2] = whole_a[:, i * WT : (i + 1) * WT]
        c = pltpu.make_async_copy(stage.at[i % 2], pa.at[:, pl.ds(i * WT, WT)], isem.at[i])
        c.start()
        if i % 2:
            pltpu.make_async_copy(stage.at[0], pa.at[:, pl.ds((i - 1) * WT, WT)], isem.at[i - 1]).wait()
            c.wait()
    att.give()
    for i in range(4, 10):
        ffn.step(i)
        if i >= 5:
            att.step(i - 5)
    for i in range(5, 10):
        att.step(i)
    (d, n), (zd, zn) = ffn.result
    def total(x, z):
        return x.astype(F32) + z.astype(F32)
    def store(i, _):
        c = pl.ds(pl.multiple_of(i * 1024, 1024), 1024)
        g_in[:, c] = total(d[:, c], zd[:, c])
        return 0
    lax.fori_loop(0, 2 * FP // 1024, store, 0)
    g_down[...] = total(n[...], zn[...])[:76]
    (a,), (za,) = att.result
    v = total(a[...], za[...])
    g_qkv[...] = v[:14, :QKV]
    g_out[...] = v[:14, QKV:]
    g_rows[...] = v
    ffn.finish()
    att.finish()


def last(attn_in, ops, pairs_):
    sds = jax.ShapeDtypeStruct
    vmem, dma = pltpu.VMEM, pltpu.SemaphoreType.DMA
    flat = [v for p in pairs_ for v in p]
    return pl.pallas_call(
        last_kernel,
        out_shape=(sds((TOK, D), F32), sds((14, QKV), F32), sds((14, D), F32), sds((16, 2 * FP), F32), sds((76, D), F32), sds((16, GATE), F32),
                   sds((DP, 2 * FP), BF), sds((FP, D), BF), sds((DP, GATE), BF),
                   sds((32, 16, 2 * FP), BF), sds((32, 80, D), BF), sds((32, 16, GATE), BF)),
        in_specs=[VM] * 10 + [ANY] + [VM] * 5 + [ANY] * 14,
        out_specs=(VM,) * 6 + (ANY,) * 6,
        scratch_shapes=[
            vmem((DP, QKV), BF), vmem((DP, D), BF), vmem((4, TOK, 256), F32), vmem((3, TOK, 256), F32), dma((2,)), dma((3,)), dma((3,)),
            vmem((HELD, 16, 2 * FP), BF), vmem((HELD, 80, D), BF), vmem((2, 16, 2 * FP), BF), vmem((2, 80, D), BF),
            vmem((31, 16, 2 * FP), BF), vmem((31, 80, D), BF),
            vmem((32, 16, GATE), BF), vmem((2, 16, GATE), BF), vmem((31, 16, GATE), BF),
            vmem((TOK, DP), BF), vmem((TOK, 2 * FP), BF), vmem((TOK, FP), BF), vmem((TOK, D), BF),
            vmem((2, DP, WT), BF), vmem((2, 640, D), BF), vmem((2, TOK, DP), BF), vmem((TOK, GATE), BF),
            dma((2 * KINDS,)), dma((2 * KINDS,)), dma((2, 4)), dma((KINDS,)), dma((KINDS,)), dma((2, 2)),
            dma((7,)), dma((4,)), dma((4,))],
        compiler_params=pltpu.CompilerParams(collective_id=1, has_side_effects=True, vmem_limit_bytes=63 * 2**20),
        name="last",
    )(*attn_in, *ops, *flat)[:6]


def per_device(ends_in, segment_ids, norm_gains, qkv_weight, qkv_bias, out_weight, in_weight, down_weight):
    section = lax.axis_index("section")
    me = lax.axis_index("ctx")
    lead = in_weight[0].reshape(14, 2, 64, 76)
    lead = jnp.pad(lead, ((0, 0), (0, 0), (0, 0), (0, 4))).reshape(14, 2 * FP)
    rows = jnp.concatenate([qkv_weight[0], out_weight[0], lead], axis=1)
    pad = lambda v, n: jnp.pad(v, (0, n - v.shape[0]))
    extra = jnp.concatenate([pad(norm_gains[0, 0], 128), pad(norm_gains[0, 1], 128), pad(qkv_bias[0], WIDE - 256)])
    wd = jnp.concatenate([rows, extra[None], pad(segment_ids.astype(BF).reshape(-1), WIDE)[None]], axis=0)
    wn = jnp.pad(down_weight[0], ((0, 4), (0, 0)))
    gd, gn = gather(wd, wn)
    gains = [gd[:, 14, 128 * i : 128 * i + 14].reshape(1, D).astype(F32) for i in (0, 1)]
    bias = gd[:, 14, 256:274].reshape(1, QKV).astype(F32)
    gathered = gd
    gd, gn = gd.reshape(DP, WIDE), gn.reshape(FP, D)
    src = jnp.arange(D)
    spread = ((src + 2 * (src // 14))[:, None] == jnp.arange(DP)[None, :]).astype(BF)

    pack_rows = lax.dynamic_slice(gathered, (4 * lax.axis_index("dp"), 15, 0), (4, 1, PACKS * ROWS))
    ids = pack_rows.reshape(4, PACKS, ROWS).transpose(1, 0, 2).reshape(PACKS, 4 * ROWS).astype(jnp.int32)
    at = jnp.arange(4 * ROWS, dtype=jnp.int32)
    own_at = me * ROWS + at[:ROWS]
    same = (segment_ids[:, 0, :, None] == ids[:, None, :]) & (at[None, None, :] <= own_at[None, :, None])
    pos = (jnp.sum(same.astype(jnp.int32), axis=2) - 1).astype(F32)
    freq = 1000000.0 ** (-jnp.arange(0, HEAD, 2, dtype=F32) / HEAD)
    angle = pos[..., None] * freq
    c, s = jnp.cos(angle), jnp.sin(angle)
    cos = jnp.concatenate([c, c, c, c], axis=-1)
    sin = jnp.concatenate([-s, s, -s, s], axis=-1)

    tables = (cos.reshape(TOK, 128), sin.reshape(TOK, 128), segment_ids.reshape(TOK, 1), ids)
    first = ends_in[0].reshape(TOK, D)
    kept, back = [], []
    h = first.astype(F32)
    for t in range(2):
        mid, a, q, kv, o = attn_fwd(h, gains[0], bias, *tables, spread, gd)
        y, y_low, b, gate, up, m = ffn_fwd(mid, gains[1], spread, gd, gn)
        kept.append((h, mid, a, q, kv, o, y, b, gate, up, m))
        if t == 0:
            h = lax.ppermute(y_low, "section", [(0, 1)]).astype(F32)
    zero = jnp.zeros_like(first)
    gy1 = jnp.where(section == 1, first, zero)
    h, mid, a, q, kv, o, y, b, gate, up, m = kept[1]
    gmid, gg1, *gu1 = ffn_bwd(gy1, mid, gains[1], spread, gate, up, gd, gn)
    gh_low, glin1, gz1, gg0, gb = attn_bwd(gmid, h, q, kv, gains[0], *tables, spread, gd)
    gy0 = lax.ppermute(gh_low, "section", [(1, 0)])
    h, mid, a, q, kv, o, _, b, gate, up, m = kept[0]
    gmid, gg, *gu0 = ffn_bwd(gy0, mid, gains[1], spread, gate, up, gd, gn)
    pick = lambda i: (kept[0][i], kept[1][i])
    gh, g_qkv, g_out, g_in, g_down, g_rows = last(
        (gmid, h, q, kv, gains[0]) + tables + (spread, gd), (glin1, gz1, gg0, gg1 + gg, gb),
        (pick(2), pick(5), pick(7), pick(10), (gu0[0], gu1[0]), (gu0[1], gu1[1]), (gy0, gy1)))
    s = 4 * lax.axis_index("dp") + me
    g_gains = lax.dynamic_slice(g_rows, (14, QKV + 14 * s), (2, 14))
    g_bias = lax.dynamic_slice(g_rows, (14, 18 * s), (1, 18))
    ends = jnp.where(section == 0, gh, y).reshape(PACKS, ROWS, D)
    g_in = g_in[:14].reshape(14, 2, 64, 80)[..., :76].reshape(14, 2 * FF)
    return ends[None, :, None], g_gains[None], g_qkv[None], g_bias, g_out[None], g_in[None], g_down[None]


def solution(mesh):
    both = ("dp", "ctx")
    ends = P("section", None, "dp", "ctx", None)
    weights = (P("section", None, both), P("section", both, None), P("section", both), P("section", both, None),
               P("section", both, None), P("section", both, None))
    return jax.shard_map(per_device, mesh=mesh, in_specs=(ends, P(None, "dp", "ctx")) + weights,
                         out_specs=(ends,) + weights, check_vma=False)
```

```python
import jax
import jax.numpy as jnp
import numpy as np
from jax import lax
from jax.experimental import pallas as pl
from jax.experimental.pallas import tpu as pltpu
from jax.sharding import PartitionSpec as P

MESH = pl.DeviceIdType.MESH
HEADS = 14
HEAD = 64
D = 896
DP = 1024
QKV = 1152
FF = 4864
FP = 5120
PACKS = 2
ROWS = 128
TOK = PACKS * ROWS
GATE = QKV + D
TILE = 1024
EPS = 1e-06
BF = jnp.bfloat16
F32 = jnp.float32
ANY = pl.BlockSpec(memory_space=pl.ANY)
VM = pl.BlockSpec(memory_space=pltpu.VMEM)


def nn(a, b):
    return jnp.dot(a, b, preferred_element_type=F32)


def nt(a, b):
    return lax.dot_general(a, b, (((1,), (1,)), ((), ())), preferred_element_type=F32)


def tn(a, b):
    return lax.dot_general(a, b, (((0,), (0,)), ((), ())), preferred_element_type=F32)


def unpad(v, spread):
    hi = v.astype(BF)
    lo = (v - hi.astype(F32)).astype(BF)
    return nt(hi, spread) + nt(lo, spread)


def rms(v):
    return lax.rsqrt(jnp.mean(v * v, axis=-1, keepdims=True) + EPS)


def rms_back(g_normed, v, gain):
    r = rms(v)
    n = v * r
    gg = g_normed * gain
    pulled = r * (gg - n * jnp.mean(gg * n, axis=-1, keepdims=True))
    return pulled, jnp.sum(g_normed * n, axis=0, keepdims=True)


def swap(u):
    width = u.shape[1]
    lane = lax.broadcasted_iota(jnp.int32, u.shape, 1)
    return jnp.where(lane % 64 < 32, pltpu.roll(u, width - 32, 1), pltpu.roll(u, 32, 1))


def wide(table, n):
    return jnp.concatenate([table] * n, axis=1)


def variants(kv):
    kv = kv.astype(F32)
    lo = lax.broadcasted_iota(jnp.int32, kv.shape, 1) < 64
    turned = pltpu.roll(kv, 64, 1)
    return [
        jnp.where(lo, kv, 0.0).astype(BF),
        jnp.where(lo, 0.0, turned).astype(BF),
        jnp.where(lo, turned, 0.0).astype(BF),
        jnp.where(lo, 0.0, kv).astype(BF),
    ]


GROUPS = ((0, 0, (0, 1, 2, 3)), (0, 1, (0, 1, 2)), (1, 0, (4, 5, 6)), (1, 1, (3, 4, 5, 6)))


def pairs(v, which):
    return jnp.concatenate([v[:, 128 * p : 128 * p + 128] for p in which], axis=0)


def allowed_mask(ids_own, ids_all, me):
    row = me * ROWS + lax.broadcasted_iota(jnp.int32, (ROWS, 4 * ROWS), 0)
    col = lax.broadcasted_iota(jnp.int32, (ROWS, 4 * ROWS), 1)
    return (ids_own == ids_all) & (col <= row)


def probs(q, k_var, mask, which):
    s = nt(pairs(q, which), k_var).reshape(len(which), ROWS, 4 * ROWS)
    s = jnp.where(mask[None], s, -1e9)
    e = jnp.exp(s - jnp.max(s, axis=-1, keepdims=True))
    p = e / jnp.sum(e, axis=-1, keepdims=True)
    return p.reshape(len(which) * ROWS, 4 * ROWS)


def greet(peers, section=None):
    barrier = pltpu.get_barrier_semaphore()
    if section is not None:
        pl.semaphore_signal(barrier, inc=1, device_id={"section": section}, device_id_type=MESH)
    for c in peers:
        pl.semaphore_signal(barrier, inc=1, device_id={"ctx": c}, device_id_type=MESH)
    pl.semaphore_wait(barrier, 3 if section is None else 4)


def attn_ahead(x, gain, bias, cos, sin, ids_own, ids_all, spread, wqkv, wout, mid, a_out, q_out, kv_out, o_out,
               kv, send, recv, me, peers):
    a = nn((x * rms(x) * gain).astype(BF), spread[...]).astype(BF)
    a_out[...] = a
    lin = nn(a, wqkv()) + bias[...]
    qk = lin[:, :1024]
    qk = qk * wide(cos[...], 8) + swap(qk) * wide(sin[...], 8)
    q = (qk[:, :D] * HEAD**-0.5).astype(BF)
    q_out[...] = q
    kv[me] = jnp.concatenate([qk[:, D:], lin[:, 1024:]], axis=1).astype(BF)
    moves = [pltpu.make_async_remote_copy(src_ref=kv.at[me], dst_ref=kv.at[me], send_sem=send.at[d], recv_sem=recv.at[d],
                                          device_id={"ctx": c}, device_id_type=MESH) for d, c in enumerate(peers)]
    for m in moves:
        m.start()
    yield
    for m in moves:
        m.wait_recv()
    for m in moves:
        m.wait_send()
    rows = []
    for pack in range(PACKS):
        here = slice(pack * ROWS, (pack + 1) * ROWS)
        mask = allowed_mask(ids_own[here, :], ids_all[pack : pack + 1, :], me)
        full = kv[:, here, :].reshape(4 * ROWS, 256)
        kv_out[pack] = full
        ks, vs = variants(full[:, :128]), variants(full[:, 128:])
        o = [jnp.zeros((ROWS, 128), F32)] * 7
        for g, par, which in GROUPS:
            p = probs(q[here], ks[2 * g + par], mask, which).astype(BF)
            part = nn(p, vs[2 * g + par])
            for i, w in enumerate(which):
                o[w] = o[w] + part[i * ROWS : (i + 1) * ROWS]
            yield
        rows.append(jnp.concatenate(o, axis=1).astype(BF))
    o = nn(jnp.concatenate(rows, axis=0), spread[...]).astype(BF)
    o_out[...] = o
    mid[...] = x + nn(o, wout())


def attn_fwd_kernel(h, gain, bias, cos, sin, ids_own, ids_all, spread, ga, mid, a_out, q_out, kv_out, o_out,
                    wqkv, wout, kv, wsem, send, recv):
    me = lax.axis_index("ctx")
    peers = [lax.rem(me + d, 4) for d in (1, 2, 3)]
    loads = [pltpu.make_async_copy(ga.at[:, pl.ds(0, QKV)], wqkv, wsem.at[0]),
             pltpu.make_async_copy(ga.at[:, pl.ds(QKV, D)], wout, wsem.at[1])]
    for c in loads:
        c.start()
    greet(peers)

    def loaded(i, ref):
        loads[i].wait()
        return ref[...]
    for _ in attn_ahead(h[...].astype(F32), gain[...], bias, cos, sin, ids_own, ids_all, spread, lambda: loaded(0, wqkv), lambda: loaded(1, wout),
                        mid, a_out, q_out, kv_out, o_out, kv, send, recv, me, peers):
        pass


def attn_fwd(h, gain, bias, cos, sin, ids_own, ids_all, spread, gd):
    sds = jax.ShapeDtypeStruct
    return pl.pallas_call(
        attn_fwd_kernel,
        out_shape=(sds((TOK, D), F32), sds((TOK, DP), BF), sds((TOK, D), BF), sds((PACKS, 4 * ROWS, 256), BF), sds((TOK, DP), BF)),
        in_specs=[VM] * 8 + [ANY],
        out_specs=(VM,) * 5,
        scratch_shapes=[pltpu.VMEM((DP, QKV), BF), pltpu.VMEM((DP, D), BF), pltpu.VMEM((4, TOK, 256), BF),
                        pltpu.SemaphoreType.DMA((2,)), pltpu.SemaphoreType.DMA((3,)), pltpu.SemaphoreType.DMA((3,))],
        compiler_params=pltpu.CompilerParams(collective_id=2, has_side_effects=True, vmem_limit_bytes=48 * 2**20),
        name="attn_fwd",
    )(h, gain, bias, cos, sin, ids_own, ids_all, spread, gd)


def attn_back(gmid, q_ref, kv_ref, cos, sin, ids_own, ids_all, spread, wout, part, got, send, recv, me, peers, load):
    gz = gmid[...].astype(BF)
    load.wait()
    go = nt(nt(gz, wout[...]).astype(BF), spread[...]).astype(BF)
    yield gz
    q = q_ref[...]
    lo = lax.broadcasted_iota(jnp.int32, (4 * ROWS, 128), 1) < 64

    def merged(e0, o0, e1, o1):
        return jnp.where(lo, e0, o1) + pltpu.roll(jnp.where(lo, e1, o0), 64, 1)

    rows = []
    for pack in range(PACKS):
        here = slice(pack * ROWS, (pack + 1) * ROWS)
        full = kv_ref[pack]
        ks, vs = variants(full[:, :128]), variants(full[:, 128:])
        mask = allowed_mask(ids_own[here, :], ids_all[pack : pack + 1, :], me)
        gq = [jnp.zeros((ROWS, 128), F32)] * 7
        gk, gv = [], []
        for n, (g, par, which) in enumerate(GROUPS):
            p = probs(q[here], ks[2 * g + par], mask, which)
            go_here = pairs(go[here], which)
            gp = nt(go_here, vs[2 * g + par])
            gv.append(tn(p.astype(BF), go_here))
            gs = (p * (gp - jnp.sum(p * gp, axis=-1, keepdims=True))).astype(BF)
            gk.append(tn(gs, pairs(q[here], which)))
            back = nn(gs, ks[2 * g + par])
            for i, w in enumerate(which):
                gq[w] = gq[w] + back[i * ROWS : (i + 1) * ROWS]
            if n == 3:
                part[:, here, :] = jnp.concatenate([merged(*gk), merged(*gv)], axis=1).reshape(4, ROWS, 256)
                rows.append(jnp.concatenate(gq, axis=1))
                if pack == PACKS - 1:
                    moves = [pltpu.make_async_remote_copy(src_ref=part.at[c], dst_ref=got.at[d], send_sem=send.at[d], recv_sem=recv.at[d],
                                                          device_id={"ctx": c}, device_id_type=MESH) for d, c in enumerate(peers)]
                    for m in moves:
                        m.start()
            yield None
    cs, sn = cos[...], sin[...]
    gq = jnp.concatenate(rows, axis=0) * HEAD**-0.5
    gq = gq * wide(cs, 7) + swap(gq * wide(sn, 7))
    for m in moves:
        m.wait_recv()
    for m in moves:
        m.wait_send()
    own = part[me] + got[0] + got[1] + got[2]
    gk = own[:, :128]
    gk = gk * cs + swap(gk * sn)
    yield jnp.concatenate([gq, gk, own[:, 128:]], axis=1).astype(BF)


def attn_bwd_kernel(gmid, h, q_ref, kv_ref, gain, cos, sin, ids_own, ids_all, spread, gd,
                    gy_next, glin_out, gz_out, ggain, gbias, wqkv, wout, part, got, gh_low, wsem, send, recv, xsem):
    me, section = lax.axis_index("ctx"), lax.axis_index("section")
    peers = [lax.rem(me + d, 4) for d in (1, 2, 3)]
    loads = [pltpu.make_async_copy(gd.at[:, pl.ds(0, QKV)], wqkv, wsem.at[0]),
             pltpu.make_async_copy(gd.at[:, pl.ds(QKV, D)], wout, wsem.at[1])]
    for c in loads:
        c.start()
    greet(peers, 1 - section)
    found = list(attn_back(gmid, q_ref, kv_ref, cos, sin, ids_own, ids_all, spread, wout, part, got, send, recv, me, peers, loads[1]))
    gz_out[...] = found[0]
    glin = found[-1]
    glin_out[...] = glin
    gbias[...] = jnp.sum(glin.astype(F32), axis=0, keepdims=True)
    loads[0].wait()
    ga = unpad(nt(glin, wqkv[...]), spread[...])
    pulled, gg = rms_back(ga, h[...].astype(F32), gain[...])
    ggain[...] = gg
    gh_low[...] = (gmid[...] + pulled).astype(BF)
    move = pltpu.make_async_remote_copy(src_ref=gh_low, dst_ref=gy_next, send_sem=xsem.at[0], recv_sem=xsem.at[1],
                                        device_id={"section": 1 - section}, device_id_type=MESH)

    @pl.when(section == 1)
    def _():
        gy_next[...] = jnp.zeros_like(gy_next)
        move.start()
        move.wait_send()

    @pl.when(section == 0)
    def _():
        move.wait_recv()


def attn_bwd(gmid, h, q, kv, gain, cos, sin, ids_own, ids_all, spread, gd):
    sds = jax.ShapeDtypeStruct
    return pl.pallas_call(
        attn_bwd_kernel,
        out_shape=(sds((TOK, D), BF), sds((TOK, QKV), BF), sds((TOK, D), BF), sds((1, D), F32), sds((1, QKV), F32)),
        in_specs=[VM] * 10 + [ANY],
        out_specs=(VM,) * 5,
        scratch_shapes=[pltpu.VMEM((DP, QKV), BF), pltpu.VMEM((DP, D), BF), pltpu.VMEM((4, TOK, 256), F32), pltpu.VMEM((3, TOK, 256), F32), pltpu.VMEM((TOK, D), BF),
                        pltpu.SemaphoreType.DMA((2,)), pltpu.SemaphoreType.DMA((3,)), pltpu.SemaphoreType.DMA((3,)), pltpu.SemaphoreType.DMA((2,))],
        compiler_params=pltpu.CompilerParams(collective_id=3, has_side_effects=True, vmem_limit_bytes=48 * 2**20),
        name="attn_bwd",
    )(gmid, h, q, kv, gain, cos, sin, ids_own, ids_all, spread, gd)


def ffn_fwd_kernel(mid, gain, spread, wg, wu, wd, y, b_out, gate, up, m_out, acc):
    i = pl.program_id(0)

    @pl.when(i == 0)
    def _():
        v = mid[...]
        b_out[...] = nn((v * rms(v) * gain[...]).astype(BF), spread[...]).astype(BF)
        acc[...] = v

    b = b_out[...]
    gt, u = nn(b, wg[...]), nn(b, wu[...])
    gate[...] = gt.astype(BF)
    up[...] = u.astype(BF)
    m = (gt * jax.nn.sigmoid(gt) * u).astype(BF)
    m_out[...] = m
    acc[...] += nn(m, wd[...])

    @pl.when(i == pl.num_programs(0) - 1)
    def _():
        y[...] = acc[...]


def whole(shape):
    return pl.BlockSpec(shape, lambda i: (0, 0))


def ffn_fwd(mid, gain, spread, gd, gn):
    sds = jax.ShapeDtypeStruct
    steps = FP // TILE
    cols = pl.BlockSpec((TOK, TILE), lambda i: (0, i))
    return pl.pallas_call(
        ffn_fwd_kernel,
        grid=(steps,),
        out_shape=(sds((TOK, D), F32), sds((TOK, DP), BF), sds((TOK, FP), BF), sds((TOK, FP), BF), sds((TOK, FP), BF)),
        in_specs=[whole((TOK, D)), whole((1, D)), whole((D, DP)),
                  pl.BlockSpec((DP, TILE), lambda i: (0, i)),
                  pl.BlockSpec((DP, TILE), lambda i: (0, steps + i)),
                  pl.BlockSpec((TILE, D), lambda i: (i, 0))],
        out_specs=(whole((TOK, D)), whole((TOK, DP)), cols, cols, cols),
        scratch_shapes=[pltpu.VMEM((TOK, D), F32)],
        compiler_params=pltpu.CompilerParams(vmem_limit_bytes=48 * 2**20),
        name="ffn_fwd",
    )(mid, gain, spread, gd, gd, gn)


def ffn_bwd_kernel(gy, mid, gain, spread, gate, up, wg, wu, wd, gmid, ggain, ggate, gup, acc):
    i = pl.program_id(0)

    @pl.when(i == 0)
    def _():
        acc[...] = jnp.zeros_like(acc)

    gm = nt(gy[...], wd[...])
    gt, u = gate[...].astype(F32), up[...].astype(F32)
    sg = jax.nn.sigmoid(gt)
    ggt = (gm * u * sg * (1.0 + gt * (1.0 - sg))).astype(BF)
    gu = (gm * gt * sg).astype(BF)
    ggate[...] = ggt
    gup[...] = gu
    acc[...] += nt(ggt, wg[...]) + nt(gu, wu[...])

    @pl.when(i == pl.num_programs(0) - 1)
    def _():
        pulled, gg = rms_back(unpad(acc[...], spread[...]), mid[...], gain[...])
        gmid[...] = gy[...].astype(F32) + pulled
        ggain[...] = gg


def ffn_bwd(gy, mid, gain, spread, gate, up, gf, gn):
    sds = jax.ShapeDtypeStruct
    steps = FP // TILE
    cols = pl.BlockSpec((TOK, TILE), lambda i: (0, i))
    return pl.pallas_call(
        ffn_bwd_kernel,
        grid=(steps,),
        out_shape=(sds((TOK, D), F32), sds((1, D), F32), sds((TOK, FP), BF), sds((TOK, FP), BF)),
        in_specs=[whole((TOK, D)), whole((TOK, D)), whole((1, D)), whole((D, DP)), cols, cols,
                  pl.BlockSpec((DP, TILE), lambda i: (0, i)),
                  pl.BlockSpec((DP, TILE), lambda i: (0, steps + i)),
                  pl.BlockSpec((TILE, D), lambda i: (i, 0))],
        out_specs=(whole((TOK, D)), whole((1, D)), cols, cols),
        scratch_shapes=[pltpu.VMEM((TOK, DP), F32)],
        compiler_params=pltpu.CompilerParams(vmem_limit_bytes=48 * 2**20),
        name="ffn_bwd",
    )(gy, mid, gain, spread, gate, up, gf, gf, gn)


def place():
    dp, ctx = lax.axis_index("dp"), lax.axis_index("ctx")
    core, zh = lax.rem(ctx, 2), ctx // 2
    y, x = dp // 4, lax.rem(dp, 4)
    one = core * y + (1 - core) * x
    two = core * x + (1 - core) * y
    return core, zh, one, two


def dp_at(core, one, two):
    return two * (4 - 3 * core) + one * (1 + 3 * core)


def ids(core, zh, one, two):
    return {"dp": dp_at(core, one, two), "ctx": 2 * zh + core}


class Gather:
    def __init__(self, where, own, held, kept, rows, send, recv, loc):
        self.core, self.zh, self.one, self.two = where
        self.own, self.held, self.kept, self.rows = own, held, kept, rows
        self.send, self.recv, self.loc = send, recv, loc
        self.hs = (self.zh, 1 - self.zh)
        self.dirs = [1 - 2 * h for h in self.hs]
        self.sib = {"dp": dp_at(self.core, self.one, self.two), "ctx": 2 * self.zh + 1 - self.core}
        self.zpart = ids(self.core, 1 - self.zh, self.one, self.two)
        self.started, self.local = [], []

    def turn(self, p):
        return lax.rem(p + 8, 4)

    def shard(self, q1, q2, h):
        return 4 * dp_at(self.core, q1, q2) + 2 * h + self.core

    def blocks(self, bufs, s):
        return [r(b, s) for r, b in zip(self.rows, bufs)]

    def copies(self, src, s, msg, dev):
        n = len(self.held)
        return [pltpu.make_async_remote_copy(src_ref=a, dst_ref=g, send_sem=self.send.at[n * msg + i],
                recv_sem=self.recv.at[n * msg + i], device_id=dev, device_id_type=MESH)
                for i, (a, g) in enumerate(zip(src, self.blocks(self.held, s)))]

    def go(self, src, s, msg, dev):
        made = self.copies(src, s, msg, dev)
        for c in made:
            c.start()
        self.started += made

    def keep(self, s, src):
        n = len(self.local)
        made = [pltpu.make_async_copy(a, g, self.loc.at[n + i]) for i, (a, g) in enumerate(zip(src, self.blocks(self.kept, s)))]
        for c in made:
            c.start()
        self.local += made

    def arrive(self, s, msg):
        src = self.blocks(self.held, s)
        for c in self.copies(src, s, msg, self.sib):
            c.wait_recv()
        self.keep(s, src)
        return src

    def pos(self, k, j, p):
        return self.turn(p + (0, -self.dirs[k], self.dirs[k], 2)[j])

    def m1(self, k, kind):
        return 1 + 3 * k + kind

    def m2(self, j, k, kind):
        return 7 + (2 * j + k) * 3 + kind

    def m3(self, j, k, t):
        return 31 + (2 * j + k) * 4 + t

    def to_one(self, k, sign):
        return ids(self.core, self.zh, self.turn(self.one + sign * self.dirs[k]), self.two)

    def to_two(self, k, sign):
        return ids(self.core, self.zh, self.one, self.turn(self.two + sign * self.dirs[k]))

    def spread(self, k, j, src):
        s = self.shard(self.pos(k, j, self.one), self.two, self.hs[k])
        self.go(src, s, self.m2(j, k, 0), self.to_two(k, 1))
        self.go(src, s, self.m2(j, k, 1), self.to_two(k, -1))
        self.go(src, s, self.m3(j, k, 0), self.sib)

    def first(self, k, src):
        s = self.shard(self.one, self.two, self.hs[k])
        self.go(src, s, self.m1(k, 0), self.to_one(k, 1))
        self.go(src, s, self.m1(k, 1), self.to_one(k, -1))
        self.spread(k, 0, src)

    def run(self):
        one, two, hs = self.one, self.two, self.hs
        own = self.shard(one, two, self.zh)
        n = len(self.local)
        made = [pltpu.make_async_copy(a, g, self.loc.at[n + i]) for i, (a, g) in enumerate(zip(self.own, self.blocks(self.held, own)))]
        for c in made:
            c.start()
        self.local += [None] * len(made)
        self.go(self.own, own, 0, self.zpart)
        self.first(0, self.own)
        yield
        self.first(1, self.arrive(self.shard(one, two, hs[1]), 0))
        yield
        for k in (0, 1):
            s = self.shard(self.pos(k, 1, one), two, hs[k])
            src = self.arrive(s, self.m1(k, 0))
            self.go(src, s, self.m1(k, 2), self.to_one(k, 1))
            self.spread(k, 1, src)
            yield
            self.spread(k, 2, self.arrive(self.shard(self.pos(k, 2, one), two, hs[k]), self.m1(k, 1)))
            yield
        for k in (0, 1):
            self.spread(k, 3, self.arrive(self.shard(self.pos(k, 3, one), two, hs[k]), self.m1(k, 2)))
            yield
        for j in range(5):
            for k in (0, 1):
                if j < 4:
                    q1 = self.pos(k, j, one)
                    s = self.shard(q1, self.pos(k, 1, two), hs[k])
                    src = self.arrive(s, self.m2(j, k, 0))
                    self.go(src, s, self.m2(j, k, 2), self.to_two(k, 1))
                    self.go(src, s, self.m3(j, k, 1), self.sib)
                    yield
                    s = self.shard(q1, self.pos(k, 2, two), hs[k])
                    self.go(self.arrive(s, self.m2(j, k, 1)), s, self.m3(j, k, 2), self.sib)
                    yield
                if j > 0:
                    s = self.shard(self.pos(k, j - 1, one), self.pos(k, 3, two), hs[k])
                    self.go(self.arrive(s, self.m2(j - 1, k, 2)), s, self.m3(j - 1, k, 3), self.sib)
                    yield
        oc, o1, o2 = 1 - self.core, two, one
        for j in range(4):
            for k in (0, 1):
                for t in range(4):
                    s = 4 * dp_at(oc, self.pos(k, j, o1), self.pos(k, t, o2)) + 2 * hs[k] + oc
                    self.arrive(s, self.m3(j, k, t))
                yield
        for c in made:
            c.wait()
        self.keep(own, self.blocks(self.held, own))

    def finish(self):
        for c in self.started:
            c.wait_send()
        for c in self.local:
            if c is not None:
                c.wait()


FT = 512
BESIDE = 1
MEET = (8, 16, 24, 30)


def first_kernel(x, ids_own, spread, bias_at, bias_mask, rope, wa, wf, wn,
                 ga, gf, gn, gains, bias, cos, sin, ids_all, mid, a_out, q_out, kv_out, o_out, y, b_out, gate, up, m_out, h_next,
                 va, vf, vn, kv, acc, y_low, st_g, st_u, st_m, asend, arecv, aloc, fsend, frecv, floc, ksend, krecv, osem, xsem):
    section, me = lax.axis_index("section"), lax.axis_index("ctx")
    dp = lax.axis_index("dp")
    where = core, zh, one, two = place()
    turn = lambda p: lax.rem(p + 8, 4)
    sib = {"dp": dp_at(core, one, two), "ctx": 2 * zh + 1 - core}
    barrier = pltpu.get_barrier_semaphore()
    for other in (sib, ids(core, 1 - zh, one, two), ids(1 - core, 1 - zh, two, one), {"section": 1 - section},
                  ids(core, zh, turn(one + 1), two), ids(core, zh, turn(one - 1), two),
                  ids(core, zh, one, turn(two + 1)), ids(core, zh, one, turn(two - 1))):
        pl.semaphore_signal(barrier, inc=1, device_id=other, device_id_type=MESH)
    pl.semaphore_wait(barrier, 8)
    of16 = lambda b, s: b.at[pl.ds(pl.multiple_of(16 * s, 16), 16)]
    of80 = lambda b, s: b.at[pl.ds(pl.multiple_of(80 * s, 16), 80)]
    att = Gather(where, (wa,), (va,), (ga,), (of16,), asend, arecv, aloc)
    ffn = Gather(where, (wf, wn), (vf, vn), (gf, gn), (of16, of80), fsend, frecv, floc)
    steps, later = att.run(), ffn.run()

    def on(n):
        for _ in range(n):
            next(later, None)

    for i, _ in enumerate(steps):
        if i in MEET:
            on(1)
    block = va[:, GATE : GATE + 128]
    both = nt(block.T, spread[...])
    gains[...] = both[:2]
    lines = va[:, GATE + 128 :].astype(F32).reshape(64, 16, 128)[:, 14, :].astype(BF)
    bias[...] = jnp.sum(nn(lines, bias_at[...]) * bias_mask[...], axis=0, keepdims=True)
    parts = [va[pl.ds(pl.multiple_of(16 * (4 * dp + c), 16), 16), GATE:].astype(F32)[15:16] for c in range(4)]
    for pack in range(PACKS):
        ids_all[pack : pack + 1, :] = jnp.concatenate([p[:, pack * ROWS : (pack + 1) * ROWS] for p in parts], axis=1).astype(jnp.int32)
    at = lax.broadcasted_iota(jnp.int32, (ROWS, 4 * ROWS), 1).astype(F32)
    picks = []
    for pack in range(PACKS):
        mask = allowed_mask(ids_own[pack * ROWS : (pack + 1) * ROWS, :], ids_all[pack : pack + 1, :], me)
        pos = jnp.sum(jnp.where(mask, 1.0, 0.0), axis=1, keepdims=True) - 1.0
        picks.append(jnp.where(at == pos, 1.0, 0.0).astype(BF))
    picks = jnp.concatenate(picks, axis=0)
    table = nn(picks, rope[0]) + nn(picks, rope[1]) + nn(picks, rope[2])
    cos[...] = table[:, :128]
    sin[...] = table[:, 128:]
    on(1)
    peers = [lax.rem(me + d, 4) for d in (1, 2, 3)]
    body = attn_ahead(x[...].astype(F32), gains[0:1, :], bias, cos, sin, ids_own, ids_all, spread,
                      lambda: va[:, :QKV], lambda: va[:, QKV:GATE], mid, a_out, q_out, kv_out, o_out, kv, ksend, krecv, me, peers)
    for _ in body:
        on(BESIDE)
    v = mid[...]
    b_out[...] = nn((v * rms(v) * gains[1:2, :]).astype(BF), spread[...]).astype(BF)
    acc[...] = v
    for _ in later:
        pass

    def out(i, b):
        cols = pl.ds(i * FT if isinstance(i, int) else pl.multiple_of(i * FT, FT), FT)
        return [pltpu.make_async_copy(s.at[b], o.at[:, cols], osem.at[b, n]) for n, (s, o) in enumerate(((st_g, gate), (st_u, up), (st_m, m_out)))]

    def tile(i, b):
        c = i * FT if isinstance(i, int) else pl.multiple_of(i * FT, FT)
        gt, u = nn(b_out[...], vf[:, pl.ds(c, FT)]), nn(b_out[...], vf[:, pl.ds(FP + c, FT)])
        m = (gt * jax.nn.sigmoid(gt) * u).astype(BF)
        st_g[b], st_u[b], st_m[b] = gt.astype(BF), u.astype(BF), m
        for w in out(i, b):
            w.start()
        acc[...] += nn(m, vn[pl.ds(c, FT), :])

    for b in (0, 1):
        tile(b, b)

    def tiles(p, _):
        for b in (0, 1):
            for w in out(2 * p + b - 2, b):
                w.wait()
            tile(2 * p + b, b)
        return 0
    lax.fori_loop(1, FP // FT // 2, tiles, 0)
    y[...] = acc[...]
    y_low[...] = acc[...].astype(BF)
    move = pltpu.make_async_remote_copy(src_ref=y_low, dst_ref=h_next, send_sem=xsem.at[0], recv_sem=xsem.at[1],
                                        device_id={"section": 1 - section}, device_id_type=MESH)

    @pl.when(section == 0)
    def _():
        h_next[...] = x[...]
        move.start()
        move.wait_send()

    @pl.when(section == 1)
    def _():
        move.wait_recv()
    for b in (0, 1):
        for w in out(FP // FT - 2 + b, b):
            w.wait()
    att.finish()
    ffn.finish()


def first_tick(x, ids_own, spread, bias_at, bias_mask, rope, wa, wf, wn):
    sds = jax.ShapeDtypeStruct
    vmem, dma = pltpu.VMEM, pltpu.SemaphoreType.DMA
    wide_ff = sds((TOK, FP), BF)
    return pl.pallas_call(
        first_kernel,
        out_shape=(sds((DP, GATE + 256), BF), sds((DP, 2 * FP), BF), sds((FP, D), BF),
                   sds((2, D), F32), sds((1, QKV), F32), sds((TOK, 128), F32), sds((TOK, 128), F32), sds((PACKS, 4 * ROWS), jnp.int32),
                   sds((TOK, D), F32), sds((TOK, DP), BF), sds((TOK, D), BF), sds((PACKS, 4 * ROWS, 256), BF), sds((TOK, DP), BF),
                   sds((TOK, D), F32), sds((TOK, DP), BF), wide_ff, wide_ff, wide_ff, sds((TOK, D), BF)),
        in_specs=[VM] * 6 + [ANY] * 3,
        out_specs=(ANY,) * 3 + (VM,) * 12 + (ANY,) * 3 + (VM,),
        scratch_shapes=[
            vmem((DP, GATE + 256), BF), vmem((DP, 2 * FP), BF), vmem((FP, D), BF), vmem((4, TOK, 256), BF), vmem((TOK, D), F32), vmem((TOK, D), BF),
            vmem((2, TOK, FT), BF), vmem((2, TOK, FT), BF), vmem((2, TOK, FT), BF),
            dma((63,)), dma((63,)), dma((65,)), dma((126,)), dma((126,)), dma((130,)), dma((3,)), dma((3,)), dma((2, 3)), dma((2,))],
        compiler_params=pltpu.CompilerParams(collective_id=0, has_side_effects=True, vmem_limit_bytes=63 * 2**20),
        name="first",
    )(x, ids_own, spread, bias_at, bias_mask, rope, wa, wf, wn)


KINDS = 63
HELD = 16


class Reduction:
    def __init__(self, where, own, other, work, staged, rings, send, recv, fetched, chunks):
        self.core, self.zh, self.one, self.two = where
        self.own, self.other, self.work, self.staged, self.rings = own, other, work, staged, rings
        self.send, self.recv, self.fetched, self.chunks = send, recv, fetched, chunks
        self.hs = (self.zh, 1 - self.zh)
        self.dirs = [1 - 2 * h for h in self.hs]
        self.sib = {"dp": dp_at(self.core, self.one, self.two), "ctx": 2 * self.zh + 1 - self.core}
        self.zpart = ids(self.core, 1 - self.zh, self.one, self.two)
        self.order = [(j, k) for j in (3, 2, 1, 0) for k in (1, 0)]
        self.kinds = (3, 2, 1, 0)
        self.flat = [(j, k, t) for j, k in self.order for t in self.kinds]
        self.slots = work[0].shape[0]
        self.started, self.busy, self.sums = [], {}, {}

    def pos(self, k, j, p):
        return lax.rem(p + (0, -self.dirs[k], self.dirs[k], 2)[j] + 8, 4)

    def to_one(self, k, sign):
        return ids(self.core, self.zh, lax.rem(self.one + sign * self.dirs[k] + 8, 4), self.two)

    def to_two(self, k, sign):
        return ids(self.core, self.zh, self.one, lax.rem(self.two + sign * self.dirs[k] + 8, 4))

    def copies(self, src, dst, msg, dev):
        n = len(self.rings)
        return [pltpu.make_async_remote_copy(src_ref=a, dst_ref=g, send_sem=self.send.at[n * msg + i],
                recv_sem=self.recv.at[n * msg + i], device_id=dev, device_id_type=MESH)
                for i, (a, g) in enumerate(zip(src, dst))]

    def go(self, src, dst, msg, dev, n=None):
        made = self.copies(src, dst, msg, dev)
        for c in made:
            c.start()
        if n is None:
            self.started += made
        else:
            self.busy[n] = made

    def arrive(self, dst, msg):
        for c in self.copies(dst, dst, msg, self.sib):
            c.wait_recv()

    def add(self, dst, src):
        for d, s, step in zip(dst, src, self.chunks):
            if step is None:
                d[...] = d[...] + s[...]
                continue
            def body(i, _, d=d, s=s, step=step):
                c = pl.ds(pl.multiple_of(i * step, step), step)
                d[:, c] = d[:, c] + s[:, c]
                return 0
            lax.fori_loop(0, d.shape[1] // step, body, 0)

    def at(self, bufs, i):
        return [b.at[i] for b in bufs]

    def sslot(self, j, k, t):
        return (2 * j + k) * 4 + t

    def m2(self, j, k, kind):
        return 32 + (2 * j + k) * 3 + kind

    def m1(self, k, kind):
        return 56 + 3 * k + kind

    def ring(self, m):
        return self.at(self.rings, m - 32)

    def give(self, part=None):
        oc = 1 - self.core
        for j, k, t in self.flat:
            s = 4 * dp_at(oc, self.pos(k, j, self.two), self.pos(k, t, self.one)) + 2 * self.hs[k] + oc
            n = self.sslot(j, k, t)
            for i, c in enumerate(self.copies(self.own(s), self.at(self.other, n), n, self.sib)):
                if part in (None, i):
                    c.start()
                    self.started.append(c)

    def fetch(self, n):
        j, k, t = self.flat[n]
        s = 4 * dp_at(self.core, self.pos(k, j, self.one), self.pos(k, t, self.two)) + 2 * self.hs[k] + self.core
        got = self.at(self.other, self.sslot(j, k, t))
        b = n % 2
        out = []
        for i in range(len(self.rings)):
            out.append(pltpu.make_async_copy(self.own(s)[i], self.work[i].at[n % self.slots], self.fetched.at[b, 2 * i]))
            out.append(pltpu.make_async_copy(got[i], self.staged[i].at[b], self.fetched.at[b, 2 * i + 1]))
        return out

    def begin(self, n):
        for c in self.busy.pop(n - self.slots, ()):
            c.wait_send()
        self.arrive(self.at(self.other, self.sslot(*self.flat[n])), self.sslot(*self.flat[n]))
        for c in self.fetch(n):
            c.start()

    def piece(self, n):
        if n == 0:
            self.begin(0)
        if n + 1 < 32:
            self.begin(n + 1)
        for c in self.fetch(n):
            c.wait()
        here = self.at(self.work, n % self.slots)
        self.add(here, self.at(self.staged, n % 2))
        self.sums[self.flat[n]] = (here, n)
        return here

    def two_start(self, g):
        j, k = self.order[g]
        for i, t in enumerate(self.kinds):
            n = 4 * g + i
            here = self.piece(n)
            if t == 3:
                self.go(here, self.ring(self.m2(j, k, 2)), self.m2(j, k, 2), self.to_two(k, -1), n)
            if t == 2:
                self.go(here, self.ring(self.m2(j, k, 1)), self.m2(j, k, 1), self.to_two(k, 1), n)

    def two_mid(self, g):
        j, k = self.order[g]
        here, n = self.sums[j, k, 1]
        got = self.ring(self.m2(j, k, 2))
        self.arrive(got, self.m2(j, k, 2))
        self.add(here, got)
        self.go(here, self.ring(self.m2(j, k, 0)), self.m2(j, k, 0), self.to_two(k, -1), n)

    def two_end(self, g):
        j, k = self.order[g]
        here, n = self.sums[j, k, 0]
        for kind in (1, 0):
            got = self.ring(self.m2(j, k, kind))
            self.arrive(got, self.m2(j, k, kind))
            self.add(here, got)
        if j == 3:
            self.go(here, self.ring(self.m1(k, 2)), self.m1(k, 2), self.to_one(k, -1), n)
        if j == 2:
            self.go(here, self.ring(self.m1(k, 1)), self.m1(k, 1), self.to_one(k, 1), n)
        if j == 1:
            got = self.ring(self.m1(k, 2))
            self.arrive(got, self.m1(k, 2))
            self.add(here, got)
            self.go(here, self.ring(self.m1(k, 0)), self.m1(k, 0), self.to_one(k, -1), n)
        if j == 0:
            for kind in (1, 0):
                got = self.ring(self.m1(k, kind))
                self.arrive(got, self.m1(k, kind))
                self.add(here, got)
            if k == 1:
                self.go(here, self.ring(62), 62, self.zpart, n)
            else:
                got = self.ring(62)
                self.arrive(got, 62)
                self.result = (here, got)

    def step(self, i):
        if i < 8:
            self.two_start(i)
        if 0 <= i - 1 < 8:
            self.two_mid(i - 1)
        if 0 <= i - 2 < 8:
            self.two_end(i - 2)

    def finish(self):
        for c in self.started:
            c.wait_send()
        for made in self.busy.values():
            for c in made:
                c.wait_send()


WT = 512


def last_kernel(*refs):
    attn_in, ops, rest = refs[:11], refs[11:27], refs[27:]
    glin1, gz1, gg0_in, gg1_in, gb_in = ops[:5]
    a2, o2 = ops[5:7], ops[7:9]
    b2, m2, gate2, up2, gy2 = refs[20:22], refs[22:24], refs[24:26], refs[26:28], refs[28:30]
    (gh, g_qkv, g_out, g_in, g_down, g_rows, pd, pn, pa, hd, hn, ha) = refs[30:42]
    (wqkv, wout, part, got, wsem, asend, arecv, work_d, work_n, st_d, st_n, ring_d, ring_n, work_a, st_a, ring_a,
     lhs, rhs, vm, vgy, stage, stage_n, left, right, fsend, frecv, ffet, csend, crecv, cfet, psem, ssem, isem) = refs[42:]
    section, me = lax.axis_index("section"), lax.axis_index("ctx")
    where = core, zh, one, two = place()
    turn = lambda p: lax.rem(p + 8, 4)
    sib = {"dp": dp_at(core, one, two), "ctx": 2 * zh + 1 - core}
    zpart = ids(core, 1 - zh, one, two)
    diagonal = ids(1 - core, 1 - zh, two, one)
    barrier = pltpu.get_barrier_semaphore()
    for other in (sib, zpart, diagonal, ids(core, zh, turn(one + 1), two), ids(core, zh, turn(one - 1), two),
                  ids(core, zh, one, turn(two + 1)), ids(core, zh, one, turn(two - 1))):
        pl.semaphore_signal(barrier, inc=1, device_id=other, device_id_type=MESH)

    def mine(pairs_):
        for t in (0, 1):
            @pl.when(section == t)
            def _(t=t):
                for i, (src, dst, sem) in enumerate(pairs_):
                    pltpu.make_async_copy(src[t], dst, sem).start()

    def mine_wait(pairs_):
        for t in (0, 1):
            @pl.when(section == t)
            def _(t=t):
                for i, (src, dst, sem) in enumerate(pairs_):
                    pltpu.make_async_copy(src[t], dst, sem).wait()

    first = [(b2, lhs, psem.at[0]), (gate2, rhs.at[:, pl.ds(0, FP)], psem.at[1]), (up2, rhs.at[:, pl.ds(FP, FP)], psem.at[2])]
    second = [(m2, vm, psem.at[3]), (gy2, vgy, psem.at[4]), (a2, left.at[0], psem.at[5]), (o2, left.at[1], psem.at[6])]
    mine(second)
    mine(first)
    gmid, h, q_ref, kv_ref, gain, cos, sin, ids_own, ids_all, spread, gd = attn_in
    loads = [pltpu.make_async_copy(gd.at[:, pl.ds(0, QKV)], wqkv, wsem.at[0]),
             pltpu.make_async_copy(gd.at[:, pl.ds(QKV, D)], wout, wsem.at[1])]
    for c in loads:
        c.start()
    mine_wait(second)
    def write_n(i, b):
        at = i * 640 if isinstance(i, int) else pl.multiple_of(i * 640, 640)
        return pltpu.make_async_copy(stage_n.at[b], pn.at[pl.ds(at, 640)], ssem.at[2 + b])

    def down(i, b):
        at = i * 640 if isinstance(i, int) else pl.multiple_of(i * 640, 640)
        stage_n[b] = tn(vm[:, pl.ds(at, 640)], vgy[...]).astype(BF)
        write_n(i, b).start()

    for b in (0, 1):
        down(b, b)

    def downs(p, _):
        for b in (0, 1):
            write_n(2 * p + b - 2, b).wait()
            down(2 * p + b, b)
        return 0
    lax.fori_loop(1, FP // 1280, downs, 0)
    for b in (0, 1):
        write_n(FP // 640 - 2 + b, b).wait()
    pl.semaphore_wait(barrier, 7)

    def own_f(s):
        return pd.at[pl.ds(pl.multiple_of(16 * s, 16), 16)], pn.at[pl.ds(pl.multiple_of(80 * s, 16), 80)]

    def own_a(s):
        return (pa.at[pl.ds(pl.multiple_of(16 * s, 16), 16)],)

    ffn = Reduction(where, own_f, (hd, hn), (work_d, work_n), (st_d, st_n), (ring_d, ring_n), fsend, frecv, ffet, (1024, None))
    att = Reduction(where, own_a, (ha,), (work_a,), (st_a,), (ring_a,), csend, crecv, cfet, (None,))
    ffn.give(1)
    mine_wait(first)
    lt = lhs[...].T

    def write(i, b):
        at = i * WT if isinstance(i, int) else pl.multiple_of(i * WT, WT)
        return pltpu.make_async_copy(stage.at[b], pd.at[:, pl.ds(at, WT)], ssem.at[b])

    def tile(i, b):
        at = i * WT if isinstance(i, int) else pl.multiple_of(i * WT, WT)
        stage[b] = nn(lt, rhs[:, pl.ds(at, WT)]).astype(BF)
        write(i, b).start()

    steps = 2 * FP // WT
    for b in (0, 1):
        tile(b, b)

    def tiles(p, _):
        for b in (0, 1):
            write(2 * p + b - 2, b).wait()
            tile(2 * p + b, b)
        return 0
    lax.fori_loop(1, steps // 2, tiles, 0)
    for b in (0, 1):
        write(steps - 2 + b, b).wait()
    ffn.give(0)

    peers = [lax.rem(me + d, 4) for d in (1, 2, 3)]
    body = attn_back(gmid, q_ref, kv_ref, cos, sin, ids_own, ids_all, spread, wout, part, got, asend, arecv, me, peers, loads[1])
    gz = next(body)

    def run(n):
        for _ in range(n):
            next(body)

    ffn.step(0)
    run(2)
    ffn.step(1)
    run(3)
    ffn.step(2)
    run(3)
    ffn.step(3)
    glin = next(body)
    loads[0].wait()
    ga = unpad(nt(glin, wqkv[...]), spread[...])
    pulled, gg0 = rms_back(ga, h[...].astype(F32), gain[...])
    gh[...] = gmid[...] + pulled
    gb = jnp.sum(glin.astype(F32), axis=0, keepdims=True) + gb_in[...]
    gg0 = gg0 + gg0_in[...]
    right[:, :QKV] = glin + glin1[...]
    right[:, QKV:] = gz + gz1[...]
    line = lax.broadcasted_iota(jnp.int32, (64, 16, 1), 1)
    mixed = tn(left[0], right[:, :QKV]).reshape(64, 16, QKV)
    stage_a = [mixed + jnp.where(line == 14, gb[None], 0.0)]
    mixed = tn(left[1], right[:, QKV:]).reshape(64, 16, D)
    stage_a.append(mixed + jnp.where(line == 14, gg0[None], 0.0) + jnp.where(line == 15, gg1_in[...][None], 0.0))
    whole_a = jnp.concatenate([v.reshape(DP, -1) for v in stage_a], axis=1).astype(BF)
    for i in range(4):
        stage[i % 2] = whole_a[:, i * WT : (i + 1) * WT]
        c = pltpu.make_async_copy(stage.at[i % 2], pa.at[:, pl.ds(i * WT, WT)], isem.at[i])
        c.start()
        if i % 2:
            pltpu.make_async_copy(stage.at[0], pa.at[:, pl.ds((i - 1) * WT, WT)], isem.at[i - 1]).wait()
            c.wait()
    att.give()
    for i in range(4, 10):
        ffn.step(i)
        for n in range(2 * (i - 4), min(2 * (i - 4) + 2, 10)):
            att.step(n)
    (d, n), (zd, zn) = ffn.result
    def total(x, z):
        return x.astype(F32) + z.astype(F32)
    def store(i, _):
        c = pl.ds(pl.multiple_of(i * 1024, 1024), 1024)
        g_in[:, c] = total(d[:, c], zd[:, c])
        return 0
    lax.fori_loop(0, 2 * FP // 1024, store, 0)
    g_down[...] = total(n[...], zn[...])[:76]
    (a,), (za,) = att.result
    v = total(a[...], za[...])
    g_qkv[...] = v[:14, :QKV]
    g_out[...] = v[:14, QKV:]
    g_rows[...] = v
    ffn.finish()
    att.finish()


def last(attn_in, ops, pairs_):
    sds = jax.ShapeDtypeStruct
    vmem, dma = pltpu.VMEM, pltpu.SemaphoreType.DMA
    flat = [v for p in pairs_ for v in p]
    return pl.pallas_call(
        last_kernel,
        out_shape=(sds((TOK, D), F32), sds((14, QKV), F32), sds((14, D), F32), sds((16, 2 * FP), F32), sds((76, D), F32), sds((16, GATE), F32),
                   sds((DP, 2 * FP), BF), sds((FP, D), BF), sds((DP, GATE), BF),
                   sds((32, 16, 2 * FP), BF), sds((32, 80, D), BF), sds((32, 16, GATE), BF)),
        in_specs=[VM] * 10 + [ANY] + [VM] * 5 + [ANY] * 14,
        out_specs=(VM,) * 6 + (ANY,) * 6,
        scratch_shapes=[
            vmem((DP, QKV), BF), vmem((DP, D), BF), vmem((4, TOK, 256), F32), vmem((3, TOK, 256), F32), dma((2,)), dma((3,)), dma((3,)),
            vmem((HELD, 16, 2 * FP), BF), vmem((HELD, 80, D), BF), vmem((2, 16, 2 * FP), BF), vmem((2, 80, D), BF),
            vmem((31, 16, 2 * FP), BF), vmem((31, 80, D), BF),
            vmem((32, 16, GATE), BF), vmem((2, 16, GATE), BF), vmem((31, 16, GATE), BF),
            vmem((TOK, DP), BF), vmem((TOK, 2 * FP), BF), vmem((TOK, FP), BF), vmem((TOK, D), BF),
            vmem((2, DP, WT), BF), vmem((2, 640, D), BF), vmem((2, TOK, DP), BF), vmem((TOK, GATE), BF),
            dma((2 * KINDS,)), dma((2 * KINDS,)), dma((2, 4)), dma((KINDS,)), dma((KINDS,)), dma((2, 2)),
            dma((7,)), dma((4,)), dma((4,))],
        compiler_params=pltpu.CompilerParams(collective_id=1, has_side_effects=True, vmem_limit_bytes=63 * 2**20),
        name="last",
    )(*attn_in, *ops, *flat)[:6]


def per_device(ends_in, segment_ids, norm_gains, qkv_weight, qkv_bias, out_weight, in_weight, down_weight):
    section = lax.axis_index("section")
    me = lax.axis_index("ctx")
    lead = in_weight[0].reshape(14, 2, 64, 76)
    wf = jnp.pad(lead, ((0, 2), (0, 0), (0, 0), (0, 4))).reshape(16, 2 * FP)
    wn = jnp.pad(down_weight[0], ((0, 4), (0, 0)))
    side = jnp.pad(norm_gains[0].T, ((0, 0), (0, 254)))
    rows = jnp.concatenate([qkv_weight[0], out_weight[0], side], axis=1)
    bias_row = jnp.pad(qkv_bias[0], (GATE + 128, 128 - 18))
    ids_row = jnp.pad(segment_ids.astype(BF).reshape(-1), (GATE, 0))
    wa = jnp.concatenate([rows, bias_row[None], ids_row[None]], axis=0)
    src = np.arange(D)
    spread = jnp.asarray(src[:, None] + 2 * (src[:, None] // 14) == np.arange(DP)[None], BF)
    col = np.arange(QKV)
    bias_at = jnp.asarray(np.arange(128)[:, None] == col[None] % 18, BF)
    bias_mask = jnp.asarray(np.arange(64)[:, None] == col[None] // 18, F32)
    freq = np.float32(1000000.0) ** (-np.arange(0, HEAD, 2, dtype=np.float32) / HEAD)
    angle = (np.arange(4 * ROWS, dtype=np.float32)[:, None] * freq).astype(np.float64)
    c, s = np.cos(angle), np.sin(angle)
    table = np.concatenate([c, c, c, c, -s, s, -s, s], axis=1).astype(np.float32)
    terms = []
    for _ in range(3):
        terms.append(table.astype(BF))
        table = table - terms[-1].astype(np.float32)
    rope = jnp.asarray(np.stack(terms))
    first = ends_in[0].reshape(TOK, D)
    ids_own = segment_ids.reshape(TOK, 1)
    ga, gf, gn, gain2, bias, cos, sin, ids_all, mid, a, q, kv, o, y, b, gate, up, m, h1 = first_tick(
        first, ids_own, spread, bias_at, bias_mask, rope, wa, wf, wn)
    gains = (gain2[0:1], gain2[1:2])
    tables = (cos, sin, ids_own, ids_all)
    kept = [(first, mid, a, q, kv, o, y, b, gate, up, m)]
    mid, a, q, kv, o = attn_fwd(h1, gains[0], bias, *tables, spread, ga)
    y, b, gate, up, m = ffn_fwd(mid, gains[1], spread, gf, gn)
    kept.append((h1, mid, a, q, kv, o, y, b, gate, up, m))
    zero = jnp.zeros_like(first)
    gy1 = jnp.where(section == 1, first, zero)
    h, mid, a, q, kv, o, y, b, gate, up, m = kept[1]
    gmid, gg1, *gu1 = ffn_bwd(gy1, mid, gains[1], spread, gate, up, gf, gn)
    gy0, glin1, gz1, gg0, gb = attn_bwd(gmid, h, q, kv, gains[0], *tables, spread, ga)
    h, mid, a, q, kv, o, _, b, gate, up, m = kept[0]
    gmid, gg, *gu0 = ffn_bwd(gy0, mid, gains[1], spread, gate, up, gf, gn)
    pick = lambda i: (kept[0][i], kept[1][i])
    gh, g_qkv, g_out, g_in, g_down, g_rows = last(
        (gmid, h, q, kv, gains[0]) + tables + (spread, ga), (glin1, gz1, gg0, gg1 + gg, gb),
        (pick(2), pick(5), pick(7), pick(10), (gu0[0], gu1[0]), (gu0[1], gu1[1]), (gy0, gy1)))
    s = 4 * lax.axis_index("dp") + me
    g_gains = lax.dynamic_slice(g_rows, (14, QKV + 14 * s), (2, 14))
    g_bias = lax.dynamic_slice(g_rows, (14, 18 * s), (1, 18))
    ends = jnp.where(section == 0, gh, y).reshape(PACKS, ROWS, D)
    g_in = g_in[:14].reshape(14, 2, 64, 80)[..., :76].reshape(14, 2 * FF)
    return ends[None, :, None], g_gains[None], g_qkv[None], g_bias, g_out[None], g_in[None], g_down[None]


def solution(mesh):
    both = ("dp", "ctx")
    ends = P("section", None, "dp", "ctx", None)
    weights = (P("section", None, both), P("section", both, None), P("section", both), P("section", both, None),
               P("section", both, None), P("section", both, None))
    return jax.shard_map(per_device, mesh=mesh, in_specs=(ends, P(None, "dp", "ctx")) + weights,
                         out_specs=(ends,) + weights, check_vma=False)
```

```python
import jax
import jax.numpy as jnp
import numpy as np
from jax import lax
from jax.experimental import pallas as pl
from jax.experimental.pallas import tpu as pltpu
from jax.sharding import PartitionSpec as P

MESH = pl.DeviceIdType.MESH
HEADS = 14
HEAD = 64
D = 896
DP = 1024
QKV = 1152
FF = 4864
FP = 5120
PACKS = 2
ROWS = 128
TOK = PACKS * ROWS
GATE = QKV + D
TILE = 1024
EPS = 1e-06
BF = jnp.bfloat16
F32 = jnp.float32
ANY = pl.BlockSpec(memory_space=pl.ANY)
VM = pl.BlockSpec(memory_space=pltpu.VMEM)


def nn(a, b):
    return jnp.dot(a, b, preferred_element_type=F32)


def nt(a, b):
    return lax.dot_general(a, b, (((1,), (1,)), ((), ())), preferred_element_type=F32)


def tn(a, b):
    return lax.dot_general(a, b, (((0,), (0,)), ((), ())), preferred_element_type=F32)


def unpad(v, spread):
    hi = v.astype(BF)
    lo = (v - hi.astype(F32)).astype(BF)
    return nt(hi, spread) + nt(lo, spread)


def rms(v):
    return lax.rsqrt(jnp.mean(v * v, axis=-1, keepdims=True) + EPS)


def rms_back(g_normed, v, gain):
    r = rms(v)
    n = v * r
    gg = g_normed * gain
    pulled = r * (gg - n * jnp.mean(gg * n, axis=-1, keepdims=True))
    return pulled, jnp.sum(g_normed * n, axis=0, keepdims=True)


def swap(u):
    width = u.shape[1]
    lane = lax.broadcasted_iota(jnp.int32, u.shape, 1)
    return jnp.where(lane % 64 < 32, pltpu.roll(u, width - 32, 1), pltpu.roll(u, 32, 1))


def wide(table, n):
    return jnp.concatenate([table] * n, axis=1)


def variants(kv):
    kv = kv.astype(F32)
    lo = lax.broadcasted_iota(jnp.int32, kv.shape, 1) < 64
    turned = pltpu.roll(kv, 64, 1)
    return [
        jnp.where(lo, kv, 0.0).astype(BF),
        jnp.where(lo, 0.0, turned).astype(BF),
        jnp.where(lo, turned, 0.0).astype(BF),
        jnp.where(lo, 0.0, kv).astype(BF),
    ]


GROUPS = ((0, 0, (0, 1, 2, 3)), (0, 1, (0, 1, 2)), (1, 0, (4, 5, 6)), (1, 1, (3, 4, 5, 6)))


def pairs(v, which):
    return jnp.concatenate([v[:, 128 * p : 128 * p + 128] for p in which], axis=0)


def allowed_mask(ids_own, ids_all, me):
    row = me * ROWS + lax.broadcasted_iota(jnp.int32, (ROWS, 4 * ROWS), 0)
    col = lax.broadcasted_iota(jnp.int32, (ROWS, 4 * ROWS), 1)
    return (ids_own == ids_all) & (col <= row)


def probs(q, k_var, mask, which):
    s = nt(pairs(q, which), k_var).reshape(len(which), ROWS, 4 * ROWS)
    s = jnp.where(mask[None], s, -1e9)
    e = jnp.exp(s - jnp.max(s, axis=-1, keepdims=True))
    p = e / jnp.sum(e, axis=-1, keepdims=True)
    return p.reshape(len(which) * ROWS, 4 * ROWS)


def greet(peers, section=None):
    barrier = pltpu.get_barrier_semaphore()
    if section is not None:
        pl.semaphore_signal(barrier, inc=1, device_id={"section": section}, device_id_type=MESH)
    for c in peers:
        pl.semaphore_signal(barrier, inc=1, device_id={"ctx": c}, device_id_type=MESH)
    pl.semaphore_wait(barrier, 3 if section is None else 4)


def attn_ahead(x, gain, bias, cos, sin, ids_own, ids_all, spread, wqkv, wout, mid, a_out, q_out, kv_out, o_out,
               kv, send, recv, me, peers):
    a = nn((x * rms(x) * gain).astype(BF), spread[...]).astype(BF)
    a_out[...] = a
    lin = nn(a, wqkv()) + bias[...]
    qk = lin[:, :1024]
    qk = qk * wide(cos[...], 8) + swap(qk) * wide(sin[...], 8)
    q = (qk[:, :D] * HEAD**-0.5).astype(BF)
    q_out[...] = q
    kv[me] = jnp.concatenate([qk[:, D:], lin[:, 1024:]], axis=1).astype(BF)
    moves = [pltpu.make_async_remote_copy(src_ref=kv.at[me], dst_ref=kv.at[me], send_sem=send.at[d], recv_sem=recv.at[d],
                                          device_id={"ctx": c}, device_id_type=MESH) for d, c in enumerate(peers)]
    for m in moves:
        m.start()
    yield
    for m in moves:
        m.wait_recv()
    for m in moves:
        m.wait_send()
    rows = []
    for pack in range(PACKS):
        here = slice(pack * ROWS, (pack + 1) * ROWS)
        mask = allowed_mask(ids_own[here, :], ids_all[pack : pack + 1, :], me)
        full = kv[:, here, :].reshape(4 * ROWS, 256)
        kv_out[pack] = full
        ks, vs = variants(full[:, :128]), variants(full[:, 128:])
        o = [jnp.zeros((ROWS, 128), F32)] * 7
        for g, par, which in GROUPS:
            p = probs(q[here], ks[2 * g + par], mask, which).astype(BF)
            part = nn(p, vs[2 * g + par])
            for i, w in enumerate(which):
                o[w] = o[w] + part[i * ROWS : (i + 1) * ROWS]
            yield
        rows.append(jnp.concatenate(o, axis=1).astype(BF))
    o = nn(jnp.concatenate(rows, axis=0), spread[...]).astype(BF)
    o_out[...] = o
    mid[...] = x + nn(o, wout())


def attn_fwd_kernel(h, gain, bias, cos, sin, ids_own, ids_all, spread, ga, mid, a_out, q_out, kv_out, o_out,
                    wqkv, wout, kv, wsem, send, recv):
    me = lax.axis_index("ctx")
    peers = [lax.rem(me + d, 4) for d in (1, 2, 3)]
    loads = [pltpu.make_async_copy(ga.at[:, pl.ds(0, QKV)], wqkv, wsem.at[0]),
             pltpu.make_async_copy(ga.at[:, pl.ds(QKV, D)], wout, wsem.at[1])]
    for c in loads:
        c.start()
    greet(peers)

    def loaded(i, ref):
        loads[i].wait()
        return ref[...]
    for _ in attn_ahead(h[...].astype(F32), gain[...], bias, cos, sin, ids_own, ids_all, spread, lambda: loaded(0, wqkv), lambda: loaded(1, wout),
                        mid, a_out, q_out, kv_out, o_out, kv, send, recv, me, peers):
        pass


def attn_fwd(h, gain, bias, cos, sin, ids_own, ids_all, spread, gd):
    sds = jax.ShapeDtypeStruct
    return pl.pallas_call(
        attn_fwd_kernel,
        out_shape=(sds((TOK, D), F32), sds((TOK, DP), BF), sds((TOK, D), BF), sds((PACKS, 4 * ROWS, 256), BF), sds((TOK, DP), BF)),
        in_specs=[VM] * 8 + [ANY],
        out_specs=(VM,) * 5,
        scratch_shapes=[pltpu.VMEM((DP, QKV), BF), pltpu.VMEM((DP, D), BF), pltpu.VMEM((4, TOK, 256), BF),
                        pltpu.SemaphoreType.DMA((2,)), pltpu.SemaphoreType.DMA((3,)), pltpu.SemaphoreType.DMA((3,))],
        compiler_params=pltpu.CompilerParams(collective_id=2, has_side_effects=True, vmem_limit_bytes=48 * 2**20),
        name="attn_fwd",
    )(h, gain, bias, cos, sin, ids_own, ids_all, spread, gd)


def attn_back(gmid, q_ref, kv_ref, cos, sin, ids_own, ids_all, spread, wout, part, got, send, recv, me, peers, load):
    gz = gmid[...].astype(BF)
    load.wait()
    go = nt(nt(gz, wout[...]).astype(BF), spread[...]).astype(BF)
    yield gz
    q = q_ref[...]
    lo = lax.broadcasted_iota(jnp.int32, (4 * ROWS, 128), 1) < 64

    def merged(e0, o0, e1, o1):
        return jnp.where(lo, e0, o1) + pltpu.roll(jnp.where(lo, e1, o0), 64, 1)

    rows = []
    for pack in range(PACKS):
        here = slice(pack * ROWS, (pack + 1) * ROWS)
        full = kv_ref[pack]
        ks, vs = variants(full[:, :128]), variants(full[:, 128:])
        mask = allowed_mask(ids_own[here, :], ids_all[pack : pack + 1, :], me)
        gq = [jnp.zeros((ROWS, 128), F32)] * 7
        gk, gv = [], []
        for n, (g, par, which) in enumerate(GROUPS):
            p = probs(q[here], ks[2 * g + par], mask, which)
            go_here = pairs(go[here], which)
            gp = nt(go_here, vs[2 * g + par])
            gv.append(tn(p.astype(BF), go_here))
            gs = (p * (gp - jnp.sum(p * gp, axis=-1, keepdims=True))).astype(BF)
            gk.append(tn(gs, pairs(q[here], which)))
            back = nn(gs, ks[2 * g + par])
            for i, w in enumerate(which):
                gq[w] = gq[w] + back[i * ROWS : (i + 1) * ROWS]
            if n == 3:
                part[:, here, :] = jnp.concatenate([merged(*gk), merged(*gv)], axis=1).reshape(4, ROWS, 256)
                rows.append(jnp.concatenate(gq, axis=1))
                if pack == PACKS - 1:
                    moves = [pltpu.make_async_remote_copy(src_ref=part.at[c], dst_ref=got.at[d], send_sem=send.at[d], recv_sem=recv.at[d],
                                                          device_id={"ctx": c}, device_id_type=MESH) for d, c in enumerate(peers)]
                    for m in moves:
                        m.start()
            yield None
    cs, sn = cos[...], sin[...]
    gq = jnp.concatenate(rows, axis=0) * HEAD**-0.5
    gq = gq * wide(cs, 7) + swap(gq * wide(sn, 7))
    for m in moves:
        m.wait_recv()
    for m in moves:
        m.wait_send()
    own = part[me] + got[0] + got[1] + got[2]
    gk = own[:, :128]
    gk = gk * cs + swap(gk * sn)
    yield jnp.concatenate([gq, gk, own[:, 128:]], axis=1).astype(BF)


def attn_bwd_kernel(gmid, h, q_ref, kv_ref, gain, cos, sin, ids_own, ids_all, spread, gd,
                    gy_next, glin_out, gz_out, ggain, gbias, wqkv, wout, part, got, gh_low, wsem, send, recv, xsem):
    me, section = lax.axis_index("ctx"), lax.axis_index("section")
    peers = [lax.rem(me + d, 4) for d in (1, 2, 3)]
    loads = [pltpu.make_async_copy(gd.at[:, pl.ds(0, QKV)], wqkv, wsem.at[0]),
             pltpu.make_async_copy(gd.at[:, pl.ds(QKV, D)], wout, wsem.at[1])]
    for c in loads:
        c.start()
    greet(peers, 1 - section)
    found = list(attn_back(gmid, q_ref, kv_ref, cos, sin, ids_own, ids_all, spread, wout, part, got, send, recv, me, peers, loads[1]))
    gz_out[...] = found[0]
    glin = found[-1]
    glin_out[...] = glin
    gbias[...] = jnp.sum(glin.astype(F32), axis=0, keepdims=True)
    loads[0].wait()
    ga = unpad(nt(glin, wqkv[...]), spread[...])
    pulled, gg = rms_back(ga, h[...].astype(F32), gain[...])
    ggain[...] = gg
    gh_low[...] = (gmid[...] + pulled).astype(BF)
    move = pltpu.make_async_remote_copy(src_ref=gh_low, dst_ref=gy_next, send_sem=xsem.at[0], recv_sem=xsem.at[1],
                                        device_id={"section": 1 - section}, device_id_type=MESH)

    @pl.when(section == 1)
    def _():
        gy_next[...] = jnp.zeros_like(gy_next)
        move.start()
        move.wait_send()

    @pl.when(section == 0)
    def _():
        move.wait_recv()


def attn_bwd(gmid, h, q, kv, gain, cos, sin, ids_own, ids_all, spread, gd):
    sds = jax.ShapeDtypeStruct
    return pl.pallas_call(
        attn_bwd_kernel,
        out_shape=(sds((TOK, D), BF), sds((TOK, QKV), BF), sds((TOK, D), BF), sds((1, D), F32), sds((1, QKV), F32)),
        in_specs=[VM] * 10 + [ANY],
        out_specs=(VM,) * 5,
        scratch_shapes=[pltpu.VMEM((DP, QKV), BF), pltpu.VMEM((DP, D), BF), pltpu.VMEM((4, TOK, 256), F32), pltpu.VMEM((3, TOK, 256), F32), pltpu.VMEM((TOK, D), BF),
                        pltpu.SemaphoreType.DMA((2,)), pltpu.SemaphoreType.DMA((3,)), pltpu.SemaphoreType.DMA((3,)), pltpu.SemaphoreType.DMA((2,))],
        compiler_params=pltpu.CompilerParams(collective_id=3, has_side_effects=True, vmem_limit_bytes=48 * 2**20),
        name="attn_bwd",
    )(gmid, h, q, kv, gain, cos, sin, ids_own, ids_all, spread, gd)


def ffn_fwd_kernel(mid, gain, spread, wg, wu, wd, y, b_out, gate, up, m_out, acc):
    i = pl.program_id(0)

    @pl.when(i == 0)
    def _():
        v = mid[...]
        b_out[...] = nn((v * rms(v) * gain[...]).astype(BF), spread[...]).astype(BF)
        acc[...] = v

    b = b_out[...]
    gt, u = nn(b, wg[...]), nn(b, wu[...])
    gate[...] = gt.astype(BF)
    up[...] = u.astype(BF)
    m = (gt * jax.nn.sigmoid(gt) * u).astype(BF)
    m_out[...] = m
    acc[...] += nn(m, wd[...])

    @pl.when(i == pl.num_programs(0) - 1)
    def _():
        y[...] = acc[...]


def whole(shape):
    return pl.BlockSpec(shape, lambda i: (0, 0))


def ffn_fwd(mid, gain, spread, gd, gn):
    sds = jax.ShapeDtypeStruct
    steps = FP // TILE
    cols = pl.BlockSpec((TOK, TILE), lambda i: (0, i))
    return pl.pallas_call(
        ffn_fwd_kernel,
        grid=(steps,),
        out_shape=(sds((TOK, D), F32), sds((TOK, DP), BF), sds((TOK, FP), BF), sds((TOK, FP), BF), sds((TOK, FP), BF)),
        in_specs=[whole((TOK, D)), whole((1, D)), whole((D, DP)),
                  pl.BlockSpec((DP, TILE), lambda i: (0, i)),
                  pl.BlockSpec((DP, TILE), lambda i: (0, steps + i)),
                  pl.BlockSpec((TILE, D), lambda i: (i, 0))],
        out_specs=(whole((TOK, D)), whole((TOK, DP)), cols, cols, cols),
        scratch_shapes=[pltpu.VMEM((TOK, D), F32)],
        compiler_params=pltpu.CompilerParams(vmem_limit_bytes=48 * 2**20),
        name="ffn_fwd",
    )(mid, gain, spread, gd, gd, gn)


def ffn_bwd_kernel(gy, mid, gain, spread, gate, up, wg, wu, wd, gmid, ggain, ggate, gup, acc):
    i = pl.program_id(0)

    @pl.when(i == 0)
    def _():
        acc[...] = jnp.zeros_like(acc)

    gm = nt(gy[...], wd[...])
    gt, u = gate[...].astype(F32), up[...].astype(F32)
    sg = jax.nn.sigmoid(gt)
    ggt = (gm * u * sg * (1.0 + gt * (1.0 - sg))).astype(BF)
    gu = (gm * gt * sg).astype(BF)
    ggate[...] = ggt
    gup[...] = gu
    acc[...] += nt(ggt, wg[...]) + nt(gu, wu[...])

    @pl.when(i == pl.num_programs(0) - 1)
    def _():
        pulled, gg = rms_back(unpad(acc[...], spread[...]), mid[...], gain[...])
        gmid[...] = gy[...].astype(F32) + pulled
        ggain[...] = gg


def ffn_bwd(gy, mid, gain, spread, gate, up, gf, gn):
    sds = jax.ShapeDtypeStruct
    steps = FP // TILE
    cols = pl.BlockSpec((TOK, TILE), lambda i: (0, i))
    return pl.pallas_call(
        ffn_bwd_kernel,
        grid=(steps,),
        out_shape=(sds((TOK, D), F32), sds((1, D), F32), sds((TOK, FP), BF), sds((TOK, FP), BF)),
        in_specs=[whole((TOK, D)), whole((TOK, D)), whole((1, D)), whole((D, DP)), cols, cols,
                  pl.BlockSpec((DP, TILE), lambda i: (0, i)),
                  pl.BlockSpec((DP, TILE), lambda i: (0, steps + i)),
                  pl.BlockSpec((TILE, D), lambda i: (i, 0))],
        out_specs=(whole((TOK, D)), whole((1, D)), cols, cols),
        scratch_shapes=[pltpu.VMEM((TOK, DP), F32)],
        compiler_params=pltpu.CompilerParams(vmem_limit_bytes=48 * 2**20),
        name="ffn_bwd",
    )(gy, mid, gain, spread, gate, up, gf, gf, gn)


def place():
    dp, ctx = lax.axis_index("dp"), lax.axis_index("ctx")
    core, zh = lax.rem(ctx, 2), ctx // 2
    y, x = dp // 4, lax.rem(dp, 4)
    one = core * y + (1 - core) * x
    two = core * x + (1 - core) * y
    return core, zh, one, two


def dp_at(core, one, two):
    return two * (4 - 3 * core) + one * (1 + 3 * core)


def ids(core, zh, one, two):
    return {"dp": dp_at(core, one, two), "ctx": 2 * zh + core}


class Gather:
    def __init__(self, where, own, held, kept, rows, send, recv, loc):
        self.core, self.zh, self.one, self.two = where
        self.own, self.held, self.kept, self.rows = own, held, kept, rows
        self.send, self.recv, self.loc = send, recv, loc
        self.hs = (self.zh, 1 - self.zh)
        self.dirs = [1 - 2 * h for h in self.hs]
        self.sib = {"dp": dp_at(self.core, self.one, self.two), "ctx": 2 * self.zh + 1 - self.core}
        self.zpart = ids(self.core, 1 - self.zh, self.one, self.two)
        self.started, self.local = [], []

    def turn(self, p):
        return lax.rem(p + 8, 4)

    def shard(self, q1, q2, h):
        return 4 * dp_at(self.core, q1, q2) + 2 * h + self.core

    def blocks(self, bufs, s):
        return [r(b, s) for r, b in zip(self.rows, bufs)]

    def copies(self, src, s, msg, dev):
        n = len(self.held)
        return [pltpu.make_async_remote_copy(src_ref=a, dst_ref=g, send_sem=self.send.at[n * msg + i],
                recv_sem=self.recv.at[n * msg + i], device_id=dev, device_id_type=MESH)
                for i, (a, g) in enumerate(zip(src, self.blocks(self.held, s)))]

    def go(self, src, s, msg, dev):
        made = self.copies(src, s, msg, dev)
        for c in made:
            c.start()
        self.started += made

    def keep(self, s, src):
        n = len(self.local)
        made = [pltpu.make_async_copy(a, g, self.loc.at[n + i]) for i, (a, g) in enumerate(zip(src, self.blocks(self.kept, s)))]
        for c in made:
            c.start()
        self.local += made

    def arrive(self, s, msg):
        src = self.blocks(self.held, s)
        for c in self.copies(src, s, msg, self.sib):
            c.wait_recv()
        self.keep(s, src)
        return src

    def pos(self, k, j, p):
        return self.turn(p + (0, -self.dirs[k], self.dirs[k], 2)[j])

    def m1(self, k, kind):
        return 1 + 3 * k + kind

    def m2(self, j, k, kind):
        return 7 + (2 * j + k) * 3 + kind

    def m3(self, j, k, t):
        return 31 + (2 * j + k) * 4 + t

    def to_one(self, k, sign):
        return ids(self.core, self.zh, self.turn(self.one + sign * self.dirs[k]), self.two)

    def to_two(self, k, sign):
        return ids(self.core, self.zh, self.one, self.turn(self.two + sign * self.dirs[k]))

    def spread(self, k, j, src):
        s = self.shard(self.pos(k, j, self.one), self.two, self.hs[k])
        self.go(src, s, self.m2(j, k, 0), self.to_two(k, 1))
        self.go(src, s, self.m2(j, k, 1), self.to_two(k, -1))
        self.go(src, s, self.m3(j, k, 0), self.sib)

    def first(self, k, src):
        s = self.shard(self.one, self.two, self.hs[k])
        self.go(src, s, self.m1(k, 0), self.to_one(k, 1))
        self.go(src, s, self.m1(k, 1), self.to_one(k, -1))
        self.spread(k, 0, src)

    def run(self):
        one, two, hs = self.one, self.two, self.hs
        own = self.shard(one, two, self.zh)
        n = len(self.local)
        made = [pltpu.make_async_copy(a, g, self.loc.at[n + i]) for i, (a, g) in enumerate(zip(self.own, self.blocks(self.held, own)))]
        for c in made:
            c.start()
        self.local += [None] * len(made)
        self.go(self.own, own, 0, self.zpart)
        self.first(0, self.own)
        yield
        self.first(1, self.arrive(self.shard(one, two, hs[1]), 0))
        yield
        for k in (0, 1):
            s = self.shard(self.pos(k, 1, one), two, hs[k])
            src = self.arrive(s, self.m1(k, 0))
            self.go(src, s, self.m1(k, 2), self.to_one(k, 1))
            self.spread(k, 1, src)
            yield
            self.spread(k, 2, self.arrive(self.shard(self.pos(k, 2, one), two, hs[k]), self.m1(k, 1)))
            yield
        for k in (0, 1):
            self.spread(k, 3, self.arrive(self.shard(self.pos(k, 3, one), two, hs[k]), self.m1(k, 2)))
            yield
        for j in range(5):
            for k in (0, 1):
                if j < 4:
                    q1 = self.pos(k, j, one)
                    s = self.shard(q1, self.pos(k, 1, two), hs[k])
                    src = self.arrive(s, self.m2(j, k, 0))
                    self.go(src, s, self.m2(j, k, 2), self.to_two(k, 1))
                    self.go(src, s, self.m3(j, k, 1), self.sib)
                    yield
                    s = self.shard(q1, self.pos(k, 2, two), hs[k])
                    self.go(self.arrive(s, self.m2(j, k, 1)), s, self.m3(j, k, 2), self.sib)
                    yield
                if j > 0:
                    s = self.shard(self.pos(k, j - 1, one), self.pos(k, 3, two), hs[k])
                    self.go(self.arrive(s, self.m2(j - 1, k, 2)), s, self.m3(j - 1, k, 3), self.sib)
                    yield
        oc, o1, o2 = 1 - self.core, two, one
        for j in range(4):
            for k in (0, 1):
                for t in range(4):
                    s = 4 * dp_at(oc, self.pos(k, j, o1), self.pos(k, t, o2)) + 2 * hs[k] + oc
                    self.arrive(s, self.m3(j, k, t))
                yield
        for c in made:
            c.wait()
        self.keep(own, self.blocks(self.held, own))

    def finish(self):
        for c in self.started:
            c.wait_send()
        for c in self.local:
            if c is not None:
                c.wait()


FT = 512
BESIDE = 1
MEET = (8, 16, 24, 30)


def first_kernel(x, ids_own, spread, bias_at, bias_mask, rope, wa, wf, wn,
                 ga, gf, gn, gains, bias, cos, sin, ids_all, mid, a_out, q_out, kv_out, o_out, y, b_out, gate, up, m_out, h_next,
                 va, vf, vn, kv, acc, y_low, st_g, st_u, st_m, asend, arecv, aloc, fsend, frecv, floc, ksend, krecv, osem, xsem):
    section, me = lax.axis_index("section"), lax.axis_index("ctx")
    dp = lax.axis_index("dp")
    where = core, zh, one, two = place()
    turn = lambda p: lax.rem(p + 8, 4)
    sib = {"dp": dp_at(core, one, two), "ctx": 2 * zh + 1 - core}
    barrier = pltpu.get_barrier_semaphore()
    for other in (sib, ids(core, 1 - zh, one, two), ids(1 - core, 1 - zh, two, one), {"section": 1 - section},
                  ids(core, zh, turn(one + 1), two), ids(core, zh, turn(one - 1), two),
                  ids(core, zh, one, turn(two + 1)), ids(core, zh, one, turn(two - 1))):
        pl.semaphore_signal(barrier, inc=1, device_id=other, device_id_type=MESH)
    pl.semaphore_wait(barrier, 8)
    of16 = lambda b, s: b.at[pl.ds(pl.multiple_of(16 * s, 16), 16)]
    of80 = lambda b, s: b.at[pl.ds(pl.multiple_of(80 * s, 16), 80)]
    att = Gather(where, (wa,), (va,), (ga,), (of16,), asend, arecv, aloc)
    ffn = Gather(where, (wf, wn), (vf, vn), (gf, gn), (of16, of80), fsend, frecv, floc)
    steps, later = att.run(), ffn.run()

    def on(n):
        for _ in range(n):
            next(later, None)

    for i, _ in enumerate(steps):
        if i in MEET:
            on(1)
    block = va[:, GATE : GATE + 128]
    both = nt(block.T, spread[...])
    gains[...] = both[:2]
    lines = va[:, GATE + 128 :].astype(F32).reshape(64, 16, 128)[:, 14, :].astype(BF)
    bias[...] = jnp.sum(nn(lines, bias_at[...]) * bias_mask[...], axis=0, keepdims=True)
    parts = [va[pl.ds(pl.multiple_of(16 * (4 * dp + c), 16), 16), GATE:].astype(F32)[15:16] for c in range(4)]
    for pack in range(PACKS):
        ids_all[pack : pack + 1, :] = jnp.concatenate([p[:, pack * ROWS : (pack + 1) * ROWS] for p in parts], axis=1).astype(jnp.int32)
    at = lax.broadcasted_iota(jnp.int32, (ROWS, 4 * ROWS), 1).astype(F32)
    picks = []
    for pack in range(PACKS):
        mask = allowed_mask(ids_own[pack * ROWS : (pack + 1) * ROWS, :], ids_all[pack : pack + 1, :], me)
        pos = jnp.sum(jnp.where(mask, 1.0, 0.0), axis=1, keepdims=True) - 1.0
        picks.append(jnp.where(at == pos, 1.0, 0.0).astype(BF))
    picks = jnp.concatenate(picks, axis=0)
    table = nn(picks, rope[0]) + nn(picks, rope[1]) + nn(picks, rope[2])
    cos[...] = table[:, :128]
    sin[...] = table[:, 128:]
    on(1)
    peers = [lax.rem(me + d, 4) for d in (1, 2, 3)]
    body = attn_ahead(x[...].astype(F32), gains[0:1, :], bias, cos, sin, ids_own, ids_all, spread,
                      lambda: va[:, :QKV], lambda: va[:, QKV:GATE], mid, a_out, q_out, kv_out, o_out, kv, ksend, krecv, me, peers)
    for _ in body:
        on(BESIDE)
    v = mid[...]
    b_out[...] = nn((v * rms(v) * gains[1:2, :]).astype(BF), spread[...]).astype(BF)
    acc[...] = v
    for _ in later:
        pass

    def out(i, b):
        cols = pl.ds(i * FT if isinstance(i, int) else pl.multiple_of(i * FT, FT), FT)
        return [pltpu.make_async_copy(s.at[b], o.at[:, cols], osem.at[b, n]) for n, (s, o) in enumerate(((st_g, gate), (st_u, up), (st_m, m_out)))]

    def tile(i, b):
        c = i * FT if isinstance(i, int) else pl.multiple_of(i * FT, FT)
        gt, u = nn(b_out[...], vf[:, pl.ds(c, FT)]), nn(b_out[...], vf[:, pl.ds(FP + c, FT)])
        m = (gt * jax.nn.sigmoid(gt) * u).astype(BF)
        st_g[b], st_u[b], st_m[b] = gt.astype(BF), u.astype(BF), m
        for w in out(i, b):
            w.start()
        acc[...] += nn(m, vn[pl.ds(c, FT), :])

    for b in (0, 1):
        tile(b, b)

    def tiles(p, _):
        for b in (0, 1):
            for w in out(2 * p + b - 2, b):
                w.wait()
            tile(2 * p + b, b)
        return 0
    lax.fori_loop(1, FP // FT // 2, tiles, 0)
    y[...] = acc[...]
    y_low[...] = acc[...].astype(BF)
    move = pltpu.make_async_remote_copy(src_ref=y_low, dst_ref=h_next, send_sem=xsem.at[0], recv_sem=xsem.at[1],
                                        device_id={"section": 1 - section}, device_id_type=MESH)

    @pl.when(section == 0)
    def _():
        h_next[...] = x[...]
        move.start()
        move.wait_send()

    @pl.when(section == 1)
    def _():
        move.wait_recv()
    for b in (0, 1):
        for w in out(FP // FT - 2 + b, b):
            w.wait()
    att.finish()
    ffn.finish()


def first_tick(x, ids_own, spread, bias_at, bias_mask, rope, wa, wf, wn):
    sds = jax.ShapeDtypeStruct
    vmem, dma = pltpu.VMEM, pltpu.SemaphoreType.DMA
    wide_ff = sds((TOK, FP), BF)
    return pl.pallas_call(
        first_kernel,
        out_shape=(sds((DP, GATE + 256), BF), sds((DP, 2 * FP), BF), sds((FP, D), BF),
                   sds((2, D), F32), sds((1, QKV), F32), sds((TOK, 128), F32), sds((TOK, 128), F32), sds((PACKS, 4 * ROWS), jnp.int32),
                   sds((TOK, D), F32), sds((TOK, DP), BF), sds((TOK, D), BF), sds((PACKS, 4 * ROWS, 256), BF), sds((TOK, DP), BF),
                   sds((TOK, D), F32), sds((TOK, DP), BF), wide_ff, wide_ff, wide_ff, sds((TOK, D), BF)),
        in_specs=[VM] * 6 + [ANY] * 3,
        out_specs=(ANY,) * 3 + (VM,) * 12 + (ANY,) * 3 + (VM,),
        scratch_shapes=[
            vmem((DP, GATE + 256), BF), vmem((DP, 2 * FP), BF), vmem((FP, D), BF), vmem((4, TOK, 256), BF), vmem((TOK, D), F32), vmem((TOK, D), BF),
            vmem((2, TOK, FT), BF), vmem((2, TOK, FT), BF), vmem((2, TOK, FT), BF),
            dma((63,)), dma((63,)), dma((65,)), dma((126,)), dma((126,)), dma((130,)), dma((3,)), dma((3,)), dma((2, 3)), dma((2,))],
        compiler_params=pltpu.CompilerParams(collective_id=0, has_side_effects=True, vmem_limit_bytes=63 * 2**20),
        name="first",
    )(x, ids_own, spread, bias_at, bias_mask, rope, wa, wf, wn)


KINDS = 63
HELD = 16


class Reduction:
    def __init__(self, where, own, other, work, staged, rings, send, recv, fetched, chunks):
        self.core, self.zh, self.one, self.two = where
        self.own, self.other, self.work, self.staged, self.rings = own, other, work, staged, rings
        self.send, self.recv, self.fetched, self.chunks = send, recv, fetched, chunks
        self.hs = (self.zh, 1 - self.zh)
        self.dirs = [1 - 2 * h for h in self.hs]
        self.sib = {"dp": dp_at(self.core, self.one, self.two), "ctx": 2 * self.zh + 1 - self.core}
        self.zpart = ids(self.core, 1 - self.zh, self.one, self.two)
        self.order = [(j, k) for j in (3, 2, 1, 0) for k in (1, 0)]
        self.kinds = (3, 2, 1, 0)
        self.flat = [(j, k, t) for j, k in self.order for t in self.kinds]
        self.slots = work[0].shape[0]
        self.started, self.busy, self.sums = [], {}, {}

    def pos(self, k, j, p):
        return lax.rem(p + (0, -self.dirs[k], self.dirs[k], 2)[j] + 8, 4)

    def to_one(self, k, sign):
        return ids(self.core, self.zh, lax.rem(self.one + sign * self.dirs[k] + 8, 4), self.two)

    def to_two(self, k, sign):
        return ids(self.core, self.zh, self.one, lax.rem(self.two + sign * self.dirs[k] + 8, 4))

    def copies(self, src, dst, msg, dev):
        n = len(self.rings)
        return [pltpu.make_async_remote_copy(src_ref=a, dst_ref=g, send_sem=self.send.at[n * msg + i],
                recv_sem=self.recv.at[n * msg + i], device_id=dev, device_id_type=MESH)
                for i, (a, g) in enumerate(zip(src, dst))]

    def go(self, src, dst, msg, dev, n=None):
        made = self.copies(src, dst, msg, dev)
        for c in made:
            c.start()
        if n is None:
            self.started += made
        else:
            self.busy[n] = made

    def arrive(self, dst, msg):
        for c in self.copies(dst, dst, msg, self.sib):
            c.wait_recv()

    def add(self, dst, src):
        for d, s, step in zip(dst, src, self.chunks):
            if step is None:
                d[...] = d[...] + s[...]
                continue
            def body(i, _, d=d, s=s, step=step):
                c = pl.ds(pl.multiple_of(i * step, step), step)
                d[:, c] = d[:, c] + s[:, c]
                return 0
            lax.fori_loop(0, d.shape[1] // step, body, 0)

    def at(self, bufs, i):
        return [b.at[i] for b in bufs]

    def sslot(self, j, k, t):
        return (2 * j + k) * 4 + t

    def m2(self, j, k, kind):
        return 32 + (2 * j + k) * 3 + kind

    def m1(self, k, kind):
        return 56 + 3 * k + kind

    def ring(self, m):
        return self.at(self.rings, m - 32)

    def give(self, part=None):
        oc = 1 - self.core
        for j, k, t in self.flat:
            s = 4 * dp_at(oc, self.pos(k, j, self.two), self.pos(k, t, self.one)) + 2 * self.hs[k] + oc
            n = self.sslot(j, k, t)
            for i, c in enumerate(self.copies(self.own(s), self.at(self.other, n), n, self.sib)):
                if part in (None, i):
                    c.start()
                    self.started.append(c)

    def fetch(self, n):
        j, k, t = self.flat[n]
        s = 4 * dp_at(self.core, self.pos(k, j, self.one), self.pos(k, t, self.two)) + 2 * self.hs[k] + self.core
        got = self.at(self.other, self.sslot(j, k, t))
        b = n % 2
        out = []
        for i in range(len(self.rings)):
            out.append(pltpu.make_async_copy(self.own(s)[i], self.work[i].at[n % self.slots], self.fetched.at[b, 2 * i]))
            out.append(pltpu.make_async_copy(got[i], self.staged[i].at[b], self.fetched.at[b, 2 * i + 1]))
        return out

    def begin(self, n):
        for c in self.busy.pop(n - self.slots, ()):
            c.wait_send()
        self.arrive(self.at(self.other, self.sslot(*self.flat[n])), self.sslot(*self.flat[n]))
        for c in self.fetch(n):
            c.start()

    def piece(self, n):
        if n == 0:
            self.begin(0)
        if n + 1 < 32:
            self.begin(n + 1)
        for c in self.fetch(n):
            c.wait()
        here = self.at(self.work, n % self.slots)
        self.add(here, self.at(self.staged, n % 2))
        self.sums[self.flat[n]] = (here, n)
        return here

    def two_start(self, g):
        j, k = self.order[g]
        for i, t in enumerate(self.kinds):
            n = 4 * g + i
            here = self.piece(n)
            if t == 3:
                self.go(here, self.ring(self.m2(j, k, 2)), self.m2(j, k, 2), self.to_two(k, -1), n)
            if t == 2:
                self.go(here, self.ring(self.m2(j, k, 1)), self.m2(j, k, 1), self.to_two(k, 1), n)

    def two_mid(self, g):
        j, k = self.order[g]
        here, n = self.sums[j, k, 1]
        got = self.ring(self.m2(j, k, 2))
        self.arrive(got, self.m2(j, k, 2))
        self.add(here, got)
        self.go(here, self.ring(self.m2(j, k, 0)), self.m2(j, k, 0), self.to_two(k, -1), n)

    def two_end(self, g):
        j, k = self.order[g]
        here, n = self.sums[j, k, 0]
        for kind in (1, 0):
            got = self.ring(self.m2(j, k, kind))
            self.arrive(got, self.m2(j, k, kind))
            self.add(here, got)
        if j == 3:
            self.go(here, self.ring(self.m1(k, 2)), self.m1(k, 2), self.to_one(k, -1), n)
        if j == 2:
            self.go(here, self.ring(self.m1(k, 1)), self.m1(k, 1), self.to_one(k, 1), n)
        if j == 1:
            got = self.ring(self.m1(k, 2))
            self.arrive(got, self.m1(k, 2))
            self.add(here, got)
            self.go(here, self.ring(self.m1(k, 0)), self.m1(k, 0), self.to_one(k, -1), n)
        if j == 0:
            for kind in (1, 0):
                got = self.ring(self.m1(k, kind))
                self.arrive(got, self.m1(k, kind))
                self.add(here, got)
            if k == 1:
                self.go(here, self.ring(62), 62, self.zpart, n)
            else:
                got = self.ring(62)
                self.arrive(got, 62)
                self.result = (here, got)

    def step(self, i):
        if i < 8:
            self.two_start(i)
        if 0 <= i - 1 < 8:
            self.two_mid(i - 1)
        if 0 <= i - 2 < 8:
            self.two_end(i - 2)

    def finish(self):
        for c in self.started:
            c.wait_send()
        for made in self.busy.values():
            for c in made:
                c.wait_send()


WT = 512


def last_kernel(*refs):
    attn_in, ops, rest = refs[:11], refs[11:27], refs[27:]
    glin1, gz1, gg0_in, gg1_in, gb_in = ops[:5]
    a2, o2 = ops[5:7], ops[7:9]
    b2, m2, gate2, up2, gy2 = refs[20:22], refs[22:24], refs[24:26], refs[26:28], refs[28:30]
    (gh, g_qkv, g_out, g_in, g_down, g_rows, pd, pn, pa, hd, hn, ha) = refs[30:42]
    (wqkv, wout, part, got, wsem, asend, arecv, work_d, work_n, st_d, st_n, ring_d, ring_n, work_a, st_a, ring_a,
     lhs, rhs, vm, vgy, stage, stage_n, left, right, fsend, frecv, ffet, csend, crecv, cfet, psem, ssem, isem) = refs[42:]
    section, me = lax.axis_index("section"), lax.axis_index("ctx")
    where = core, zh, one, two = place()
    turn = lambda p: lax.rem(p + 8, 4)
    sib = {"dp": dp_at(core, one, two), "ctx": 2 * zh + 1 - core}
    zpart = ids(core, 1 - zh, one, two)
    diagonal = ids(1 - core, 1 - zh, two, one)
    barrier = pltpu.get_barrier_semaphore()
    for other in (sib, zpart, diagonal, ids(core, zh, turn(one + 1), two), ids(core, zh, turn(one - 1), two),
                  ids(core, zh, one, turn(two + 1)), ids(core, zh, one, turn(two - 1))):
        pl.semaphore_signal(barrier, inc=1, device_id=other, device_id_type=MESH)

    def mine(pairs_):
        for t in (0, 1):
            @pl.when(section == t)
            def _(t=t):
                for i, (src, dst, sem) in enumerate(pairs_):
                    pltpu.make_async_copy(src[t], dst, sem).start()

    def mine_wait(pairs_):
        for t in (0, 1):
            @pl.when(section == t)
            def _(t=t):
                for i, (src, dst, sem) in enumerate(pairs_):
                    pltpu.make_async_copy(src[t], dst, sem).wait()

    first = [(b2, lhs, psem.at[0]), (gate2, rhs.at[:, pl.ds(0, FP)], psem.at[1]), (up2, rhs.at[:, pl.ds(FP, FP)], psem.at[2])]
    second = [(m2, vm, psem.at[3]), (gy2, vgy, psem.at[4]), (a2, left.at[0], psem.at[5]), (o2, left.at[1], psem.at[6])]
    mine(second)
    mine(first)
    gmid, h, q_ref, kv_ref, gain, cos, sin, ids_own, ids_all, spread, gd = attn_in
    loads = [pltpu.make_async_copy(gd.at[:, pl.ds(0, QKV)], wqkv, wsem.at[0]),
             pltpu.make_async_copy(gd.at[:, pl.ds(QKV, D)], wout, wsem.at[1])]
    for c in loads:
        c.start()
    mine_wait(second)
    def write_n(i, b):
        at = i * 640 if isinstance(i, int) else pl.multiple_of(i * 640, 640)
        return pltpu.make_async_copy(stage_n.at[b], pn.at[pl.ds(at, 640)], ssem.at[2 + b])

    def down(i, b):
        at = i * 640 if isinstance(i, int) else pl.multiple_of(i * 640, 640)
        stage_n[b] = tn(vm[:, pl.ds(at, 640)], vgy[...]).astype(BF)
        write_n(i, b).start()

    for b in (0, 1):
        down(b, b)

    def downs(p, _):
        for b in (0, 1):
            write_n(2 * p + b - 2, b).wait()
            down(2 * p + b, b)
        return 0
    lax.fori_loop(1, FP // 1280, downs, 0)
    for b in (0, 1):
        write_n(FP // 640 - 2 + b, b).wait()
    pl.semaphore_wait(barrier, 7)

    def own_f(s):
        return pd.at[pl.ds(pl.multiple_of(16 * s, 16), 16)], pn.at[pl.ds(pl.multiple_of(80 * s, 16), 80)]

    def own_a(s):
        return (pa.at[pl.ds(pl.multiple_of(16 * s, 16), 16)],)

    ffn = Reduction(where, own_f, (hd, hn), (work_d, work_n), (st_d, st_n), (ring_d, ring_n), fsend, frecv, ffet, (1024, None))
    att = Reduction(where, own_a, (ha,), (work_a,), (st_a,), (ring_a,), csend, crecv, cfet, (None,))
    ffn.give(1)
    mine_wait(first)
    lt = lhs[...].T

    def write(i, b):
        at = i * WT if isinstance(i, int) else pl.multiple_of(i * WT, WT)
        return pltpu.make_async_copy(stage.at[b], pd.at[:, pl.ds(at, WT)], ssem.at[b])

    def tile(i, b):
        at = i * WT if isinstance(i, int) else pl.multiple_of(i * WT, WT)
        stage[b] = nn(lt, rhs[:, pl.ds(at, WT)]).astype(BF)
        write(i, b).start()

    steps = 2 * FP // WT
    for b in (0, 1):
        tile(b, b)

    def tiles(p, _):
        for b in (0, 1):
            write(2 * p + b - 2, b).wait()
            tile(2 * p + b, b)
        return 0
    lax.fori_loop(1, steps // 2, tiles, 0)
    for b in (0, 1):
        write(steps - 2 + b, b).wait()
    ffn.give(0)

    peers = [lax.rem(me + d, 4) for d in (1, 2, 3)]
    body = attn_back(gmid, q_ref, kv_ref, cos, sin, ids_own, ids_all, spread, wout, part, got, asend, arecv, me, peers, loads[1])
    gz = next(body)

    def run(n):
        for _ in range(n):
            next(body)

    run(1)
    ffn.step(0)
    run(2)
    ffn.step(1)
    run(2)
    ffn.step(2)
    run(3)
    ffn.step(3)
    glin = next(body)
    loads[0].wait()
    ga = unpad(nt(glin, wqkv[...]), spread[...])
    pulled, gg0 = rms_back(ga, h[...].astype(F32), gain[...])
    gh[...] = gmid[...] + pulled
    gb = jnp.sum(glin.astype(F32), axis=0, keepdims=True) + gb_in[...]
    gg0 = gg0 + gg0_in[...]
    right[:, :QKV] = glin + glin1[...]
    right[:, QKV:] = gz + gz1[...]
    line = lax.broadcasted_iota(jnp.int32, (64, 16, 1), 1)
    mixed = tn(left[0], right[:, :QKV]).reshape(64, 16, QKV)
    stage_a = [mixed + jnp.where(line == 14, gb[None], 0.0)]
    mixed = tn(left[1], right[:, QKV:]).reshape(64, 16, D)
    stage_a.append(mixed + jnp.where(line == 14, gg0[None], 0.0) + jnp.where(line == 15, gg1_in[...][None], 0.0))
    whole_a = jnp.concatenate([v.reshape(DP, -1) for v in stage_a], axis=1).astype(BF)
    for i in range(4):
        stage[i % 2] = whole_a[:, i * WT : (i + 1) * WT]
        c = pltpu.make_async_copy(stage.at[i % 2], pa.at[:, pl.ds(i * WT, WT)], isem.at[i])
        c.start()
        if i % 2:
            pltpu.make_async_copy(stage.at[0], pa.at[:, pl.ds((i - 1) * WT, WT)], isem.at[i - 1]).wait()
            c.wait()
    att.give()
    for i in range(4, 10):
        ffn.step(i)
        for n in range(2 * (i - 4), min(2 * (i - 4) + 2, 10)):
            att.step(n)
    (d, n), (zd, zn) = ffn.result
    def total(x, z):
        return x.astype(F32) + z.astype(F32)
    def store(i, _):
        c = pl.ds(pl.multiple_of(i * 1024, 1024), 1024)
        g_in[:, c] = total(d[:, c], zd[:, c])
        return 0
    lax.fori_loop(0, 2 * FP // 1024, store, 0)
    g_down[...] = total(n[...], zn[...])[:76]
    (a,), (za,) = att.result
    v = total(a[...], za[...])
    g_qkv[...] = v[:14, :QKV]
    g_out[...] = v[:14, QKV:]
    g_rows[...] = v
    ffn.finish()
    att.finish()


def last(attn_in, ops, pairs_):
    sds = jax.ShapeDtypeStruct
    vmem, dma = pltpu.VMEM, pltpu.SemaphoreType.DMA
    flat = [v for p in pairs_ for v in p]
    return pl.pallas_call(
        last_kernel,
        out_shape=(sds((TOK, D), F32), sds((14, QKV), F32), sds((14, D), F32), sds((16, 2 * FP), F32), sds((76, D), F32), sds((16, GATE), F32),
                   sds((DP, 2 * FP), BF), sds((FP, D), BF), sds((DP, GATE), BF),
                   sds((32, 16, 2 * FP), BF), sds((32, 80, D), BF), sds((32, 16, GATE), BF)),
        in_specs=[VM] * 10 + [ANY] + [VM] * 5 + [ANY] * 14,
        out_specs=(VM,) * 6 + (ANY,) * 6,
        scratch_shapes=[
            vmem((DP, QKV), BF), vmem((DP, D), BF), vmem((4, TOK, 256), F32), vmem((3, TOK, 256), F32), dma((2,)), dma((3,)), dma((3,)),
            vmem((HELD, 16, 2 * FP), BF), vmem((HELD, 80, D), BF), vmem((2, 16, 2 * FP), BF), vmem((2, 80, D), BF),
            vmem((31, 16, 2 * FP), BF), vmem((31, 80, D), BF),
            vmem((32, 16, GATE), BF), vmem((2, 16, GATE), BF), vmem((31, 16, GATE), BF),
            vmem((TOK, DP), BF), vmem((TOK, 2 * FP), BF), vmem((TOK, FP), BF), vmem((TOK, D), BF),
            vmem((2, DP, WT), BF), vmem((2, 640, D), BF), vmem((2, TOK, DP), BF), vmem((TOK, GATE), BF),
            dma((2 * KINDS,)), dma((2 * KINDS,)), dma((2, 4)), dma((KINDS,)), dma((KINDS,)), dma((2, 2)),
            dma((7,)), dma((4,)), dma((4,))],
        compiler_params=pltpu.CompilerParams(collective_id=1, has_side_effects=True, vmem_limit_bytes=63 * 2**20),
        name="last",
    )(*attn_in, *ops, *flat)[:6]


def per_device(ends_in, segment_ids, norm_gains, qkv_weight, qkv_bias, out_weight, in_weight, down_weight):
    section = lax.axis_index("section")
    me = lax.axis_index("ctx")
    lead = in_weight[0].reshape(14, 2, 64, 76)
    wf = jnp.pad(lead, ((0, 2), (0, 0), (0, 0), (0, 4))).reshape(16, 2 * FP)
    wn = jnp.pad(down_weight[0], ((0, 4), (0, 0)))
    side = jnp.pad(norm_gains[0].T, ((0, 0), (0, 254)))
    rows = jnp.concatenate([qkv_weight[0], out_weight[0], side], axis=1)
    bias_row = jnp.pad(qkv_bias[0], (GATE + 128, 128 - 18))
    ids_row = jnp.pad(segment_ids.astype(BF).reshape(-1), (GATE, 0))
    wa = jnp.concatenate([rows, bias_row[None], ids_row[None]], axis=0)
    src = np.arange(D)
    spread = jnp.asarray(src[:, None] + 2 * (src[:, None] // 14) == np.arange(DP)[None], BF)
    col = np.arange(QKV)
    bias_at = jnp.asarray(np.arange(128)[:, None] == col[None] % 18, BF)
    bias_mask = jnp.asarray(np.arange(64)[:, None] == col[None] // 18, F32)
    freq = np.float32(1000000.0) ** (-np.arange(0, HEAD, 2, dtype=np.float32) / HEAD)
    angle = (np.arange(4 * ROWS, dtype=np.float32)[:, None] * freq).astype(np.float64)
    c, s = np.cos(angle), np.sin(angle)
    table = np.concatenate([c, c, c, c, -s, s, -s, s], axis=1).astype(np.float32)
    terms = []
    for _ in range(3):
        terms.append(table.astype(BF))
        table = table - terms[-1].astype(np.float32)
    rope = jnp.asarray(np.stack(terms))
    first = ends_in[0].reshape(TOK, D)
    ids_own = segment_ids.reshape(TOK, 1)
    ga, gf, gn, gain2, bias, cos, sin, ids_all, mid, a, q, kv, o, y, b, gate, up, m, h1 = first_tick(
        first, ids_own, spread, bias_at, bias_mask, rope, wa, wf, wn)
    gains = (gain2[0:1], gain2[1:2])
    tables = (cos, sin, ids_own, ids_all)
    kept = [(first, mid, a, q, kv, o, y, b, gate, up, m)]
    mid, a, q, kv, o = attn_fwd(h1, gains[0], bias, *tables, spread, ga)
    y, b, gate, up, m = ffn_fwd(mid, gains[1], spread, gf, gn)
    kept.append((h1, mid, a, q, kv, o, y, b, gate, up, m))
    zero = jnp.zeros_like(first)
    gy1 = jnp.where(section == 1, first, zero)
    h, mid, a, q, kv, o, y, b, gate, up, m = kept[1]
    gmid, gg1, *gu1 = ffn_bwd(gy1, mid, gains[1], spread, gate, up, gf, gn)
    gy0, glin1, gz1, gg0, gb = attn_bwd(gmid, h, q, kv, gains[0], *tables, spread, ga)
    h, mid, a, q, kv, o, _, b, gate, up, m = kept[0]
    gmid, gg, *gu0 = ffn_bwd(gy0, mid, gains[1], spread, gate, up, gf, gn)
    pick = lambda i: (kept[0][i], kept[1][i])
    gh, g_qkv, g_out, g_in, g_down, g_rows = last(
        (gmid, h, q, kv, gains[0]) + tables + (spread, ga), (glin1, gz1, gg0, gg1 + gg, gb),
        (pick(2), pick(5), pick(7), pick(10), (gu0[0], gu1[0]), (gu0[1], gu1[1]), (gy0, gy1)))
    s = 4 * lax.axis_index("dp") + me
    g_gains = lax.dynamic_slice(g_rows, (14, QKV + 14 * s), (2, 14))
    g_bias = lax.dynamic_slice(g_rows, (14, 18 * s), (1, 18))
    ends = jnp.where(section == 0, gh, y).reshape(PACKS, ROWS, D)
    g_in = g_in[:14].reshape(14, 2, 64, 80)[..., :76].reshape(14, 2 * FF)
    return ends[None, :, None], g_gains[None], g_qkv[None], g_bias, g_out[None], g_in[None], g_down[None]


def solution(mesh):
    both = ("dp", "ctx")
    ends = P("section", None, "dp", "ctx", None)
    weights = (P("section", None, both), P("section", both, None), P("section", both), P("section", both, None),
               P("section", both, None), P("section", both, None))
    return jax.shard_map(per_device, mesh=mesh, in_specs=(ends, P(None, "dp", "ctx")) + weights,
                         out_specs=(ends,) + weights, check_vma=False)
```
